512 devices in a mesh: ctx: 64 (over x, z), tp: 8 (over y, core).
Axes of the slice: x: 4, y: 4, z: 16, core: 2. Of those that a mesh axis runs over, the one named last changes fastest.
Arguments:
- hidden_states: bfloat16 [8192, 8192], P('ctx', 'tp'), may hold values from -6 to 6
- select_weight: bfloat16 [8192, 2048], P('tp', 'ctx'), may hold values from -0.0625 to 0.0625
- conv_taps: float32 [4, 2048], P(None, 'tp'), may hold values from -1.5 to 1.5
- inner_input: bfloat16 [8192, 8192], P('ctx', 'tp'), may hold values from -6 to 6
- gate_input: bfloat16 [8192, 8192], P('ctx', 'tp'), may hold values from -6 to 6
- step_size: float32 [8192, 128], P('ctx', 'tp'), as said below
- decay_rate: float32 [128], P('tp'), as said below
- skip_gain: float32 [128], P('tp'), may hold values from 0.5 to 1.5
- tenant_scale: bfloat16 [16, 8192], P(None, 'tp'), may hold values from 0.099609375 to 1.8984375
- tenant_index: int32 [64], P('ctx'), may hold values from 0 to 15
- norm_gain: bfloat16 [8192], P('tp'), may hold values from 0.099609375 to 1.8984375
Outputs:
- mixer_output: bfloat16 [8192, 8192], P('ctx', 'tp')
The draws below stay inside these ranges and needn't reach their ends.
Inputs may be any that keep to these rules, and one draw needn't show every extreme that they name: `step_size`: step sizes are positive. `decay_rate`: decay rates are positive.
All inputs are finite; a program needn't handle non-finite values.
Results may differ from the reference program's by a relative error of at most 0.012.
Values may be sent and summed in bfloat16 or wider, within the bound.
No kernel may reach another device: no remote copies, remote signals or barrier semaphores. Data moves between devices by JAX's collectives and lax.ppermute only.
A program may use at most 128 MiB of HBM per device.

```python
import jax
import jax.numpy as jnp
from jax import lax

D = 8192
H = 128
P_SIZE = 64
N = 128
G = 8
K = 4
Q = 128
SEGMENT_TOKENS = 128
TENANTS = 16
TOK_DEV = 128
SEQUENCE_TOKENS = 8192


def head_rates(key, slow_share):
    key_kind, key_slow, key_fast, key_ratio = jax.random.split(key, 4)
    slow_heads = jax.random.uniform(key_kind, (H,)) < slow_share
    slow_rate = jnp.exp(jax.random.uniform(key_slow, (H,), minval=jnp.log(0.12), maxval=jnp.log(1.2))) / TOK_DEV
    fast_rate = jnp.exp(jax.random.uniform(key_fast, (H,), minval=jnp.log(1.0 / 50.0), maxval=jnp.log(1.0 / 30.0)))
    head_rate = jnp.where(slow_heads, slow_rate, fast_rate)
    gain_ratio = jnp.exp(jax.random.uniform(key_ratio, (H,), minval=jnp.log(0.5), maxval=jnp.log(2.0)))
    return (jnp.sqrt(head_rate * gain_ratio), jnp.sqrt(head_rate / gain_ratio))


def draw_decay_rate(key, part):
    slow_share = 0.5
    baseline_step, baseline_decay = head_rates(key, slow_share)
    return baseline_decay.astype(jnp.float32)


def draw_step_size(key, part):
    slow_share = 0.5
    baseline_step, baseline_decay = head_rates(key, slow_share)
    key = jax.random.fold_in(key, 7)
    noise_key, segment_key, spike_key, dropped_key = jax.random.split(key, 4)
    random_noise = jax.random.uniform(noise_key, (SEQUENCE_TOKENS, H), minval=0.5, maxval=1.5)
    segment_factor = jnp.exp(jax.random.uniform(segment_key, (SEQUENCE_TOKENS // SEGMENT_TOKENS,), minval=jnp.log(0.5), maxval=jnp.log(2.0)))
    segment_token_ids = jnp.repeat(segment_factor, SEGMENT_TOKENS)
    spike_position = jax.random.randint(spike_key, (2,), 0, SEQUENCE_TOKENS // SEGMENT_TOKENS)
    dropped_fraction = jax.random.uniform(dropped_key, (2,), minval=0.2, maxval=0.4)
    token_segment_index = jnp.arange(SEQUENCE_TOKENS) // SEGMENT_TOKENS
    lookup_counts = (token_segment_index[:, None] == spike_position[None, :]).astype(jnp.float32)
    spike_magnitude = jnp.sum(lookup_counts * (-jnp.log(1.0 - dropped_fraction))[None, :], axis=1)
    final_output = baseline_step[None, :] * random_noise * segment_token_ids[:, None] + spike_magnitude[:, None] / SEGMENT_TOKENS / baseline_decay[None, :]
    return final_output.astype(jnp.float32)


def place_ends(drawn, rng, smallest, top_value):
    place = [jax.random.randint(jax.random.fold_in(rng, axis), (), 0, length) for axis, length in enumerate(drawn.shape)]
    main_axis = drawn.shape.index(max(drawn.shape))
    next_to = place[:main_axis] + [(place[main_axis] + 1) % drawn.shape[main_axis]] + place[main_axis + 1:]
    return drawn.at[tuple(place)].set(smallest).at[tuple(next_to)].set(top_value)


def levels(own_key, dims, pieces, low, top_value):
    def one(position, shards_of):
        heights = jax.random.uniform(jax.random.fold_in(jax.random.fold_in(own_key, 6), position), (shards_of,), jnp.float32, low / len(pieces), top_value / len(pieces))
        return jnp.repeat(jnp.exp(heights), dims[position] // shards_of).reshape((-1,) + (1,) * (len(dims) - position - 1))

    level = one(*pieces[0])
    for cut in pieces[1:]:
        level = level * one(*cut)
    return level


def gaussian(key, extent, width, limit, pieces=(), kind=jnp.bfloat16):
    values = jax.random.normal(key, extent, jnp.float32) * width
    if len(pieces) > 0:
        values = levels(key, extent, pieces, -0.22, 0.18) * values
    return jnp.clip(values, min=-limit, max=limit).astype(kind)


def setup_inputs(seed: int = 0) -> dict:
    key_list = jax.random.split(jax.random.key(seed), 12)
    return {
        "hidden_states": gaussian(key_list[0], (SEQUENCE_TOKENS, D), 1.0, 6.0, ((0, 64), (1, 8))),
        "select_weight": gaussian(key_list[1], (D, 2 * G * N), D ** -0.5, 0.0625, ((0, 8), (1, 64))),
        "conv_taps": gaussian(key_list[2], (K, 2 * G * N), 0.25, 1.5, ((1, 8),), jnp.float32),
        "inner_input": gaussian(key_list[3], (SEQUENCE_TOKENS, H * P_SIZE), 1.0, 6.0, ((0, 64), (1, 8))),
        "gate_input": gaussian(key_list[4], (SEQUENCE_TOKENS, H * P_SIZE), 1.0, 6.0, ((0, 64), (1, 8))),
        "step_size": draw_step_size(jax.random.fold_in(key_list[11], 71), 0),
        "decay_rate": draw_decay_rate(jax.random.fold_in(key_list[11], 71), 0),
        "skip_gain": jnp.clip(0.5 + 1.0 * jax.random.uniform(key_list[7], (H,), jnp.float32) ** levels(key_list[7], (H,), ((0, 8),), -0.2, 0.2), 0.5, 1.5),
        "tenant_scale": jnp.clip(1.0 + 0.18 * jax.random.normal(key_list[8], (TENANTS, H * P_SIZE), jnp.float32), 0.099609375, 1.8984375).astype(jnp.bfloat16),
        "tenant_index": place_ends(jax.random.randint(key_list[9], (SEQUENCE_TOKENS // SEGMENT_TOKENS,), 0, TENANTS), jax.random.fold_in(key_list[9], 1), 0, TENANTS - 1).astype(jnp.int32),
        "norm_gain": jnp.clip(1.0 + 0.18 * jax.random.normal(key_list[10], (H * P_SIZE,), jnp.float32), 0.099609375, 1.8984375).astype(jnp.bfloat16),
    }


epsilon = 1e-05

def project_select(hidden_states, select_weight, conv_taps):
    raw_rows = jnp.dot(hidden_states, select_weight, preferred_element_type=jnp.float32)
    padded = jnp.concatenate([jnp.zeros((K - 1, raw_rows.shape[1]), jnp.float32), raw_rows], axis=0)
    length = raw_rows.shape[0]
    summed = jnp.zeros_like(raw_rows)
    for offset in range(K):
        summed = summed + conv_taps[offset][None, :] * padded[offset:offset + length]
    return jax.nn.silu(summed).astype(jnp.bfloat16)

def reference(hidden_states, select_weight, conv_taps, inner_input, gate_input, step_size, decay_rate, skip_gain, tenant_scale, tenant_index, norm_gain):
    heads_group = H // G
    span_total = SEQUENCE_TOKENS // Q
    selected = project_select(hidden_states, select_weight, conv_taps).reshape(SEQUENCE_TOKENS, G, 2, N)
    write_key = selected[:, :, 0].reshape(span_total, Q, G, N)
    read_key = selected[:, :, 1].reshape(span_total, Q, G, N)
    log_decay = -step_size * decay_rate[None, :]
    cumulative = jnp.cumsum(log_decay.reshape(span_total, Q, H), axis=1)
    tenant_tok = jnp.repeat(tenant_index, SEGMENT_TOKENS).reshape(span_total, Q)
    causal = jnp.tril(jnp.ones((Q, Q), dtype=bool))

    def span_step(state_now, inputs):
        cumul_c, wkey_c, rkey_c, inner_c, gate_c, step_c, tenant_c = inputs
        scale_rows = tenant_scale[tenant_c].astype(jnp.float32)
        scaled = (inner_c.astype(jnp.float32) * scale_rows).reshape(Q, H, P_SIZE)
        driven = (scaled * step_c[:, :, None]).astype(jnp.bfloat16)
        driven_g = driven.reshape(Q, G, heads_group, P_SIZE).astype(jnp.float32)
        scores = jnp.einsum('tgn,sgn->gts', rkey_c.astype(jnp.float32), wkey_c.astype(jnp.float32))
        cumul_gh = cumul_c.T.reshape(G, heads_group, Q)
        lag_log = cumul_gh[:, :, :, None] - cumul_gh[:, :, None, :]
        weights = jnp.where(causal, scores[:, None] * jnp.exp(jnp.where(causal, lag_log, 0.0)), 0.0).astype(jnp.bfloat16)
        within = jnp.einsum('ghts,sghp->tghp', weights.astype(jnp.float32), driven_g)
        cumul_tg = cumul_c.reshape(Q, G, heads_group)
        carried = jnp.exp(cumul_tg)[..., None] * jnp.einsum('tgn,ghpn->tghp', rkey_c.astype(jnp.float32), state_now, precision=lax.Precision.HIGHEST)
        tail_decay = jnp.exp(cumul_tg[-1][None] - cumul_tg)
        weighted = (tail_decay[..., None] * driven_g).astype(jnp.bfloat16)
        update = jnp.einsum('sghp,sgn->ghpn', weighted.astype(jnp.float32), wkey_c.astype(jnp.float32))
        next_state = jnp.exp(cumul_tg[-1])[:, :, None, None] * state_now + update
        mixture = within + carried + skip_gain.reshape(G, heads_group)[None, :, :, None] * scaled.reshape(Q, G, heads_group, P_SIZE)
        gate_vals = jax.nn.silu(gate_c.astype(jnp.float32)).reshape(Q, G, heads_group * P_SIZE)
        gated_out = mixture.reshape(Q, G, heads_group * P_SIZE) * gate_vals
        meansq = lax.optimization_barrier(jnp.mean(gated_out * gated_out, axis=-1, keepdims=True))
        normed = gated_out * lax.rsqrt(meansq + epsilon) * norm_gain.astype(jnp.float32).reshape(G, heads_group * P_SIZE)
        return (next_state, normed.reshape(Q, H * P_SIZE).astype(jnp.bfloat16))
    start_state = jnp.zeros((G, heads_group, P_SIZE, N), jnp.float32)
    inputs = (cumulative, write_key, read_key, inner_input.reshape(span_total, Q, H * P_SIZE), gate_input.reshape(span_total, Q, H * P_SIZE), step_size.reshape(span_total, Q, H), tenant_tok)
    final_state, outputs = lax.scan(span_step, start_state, inputs)
    return outputs.reshape(SEQUENCE_TOKENS, H * P_SIZE)
```

```python
import jax
import jax.numpy as jnp
from jax import lax
from jax.sharding import Mesh, PartitionSpec as P

N = 128
Q = 128
HALO = 16
EXTRA = 128
CTX = ("x", "zh", "zl")
TP = ("y", "core")

epsilon = 1e-05
bf16 = jnp.bfloat16
f32 = jnp.float32


def swap(blocks, axis):
    return lax.all_to_all(blocks, axis, 0, 0, tiled=True)


def share(block, axis):
    peers = lax.axis_size(axis)
    return swap(jnp.broadcast_to(block[None], (peers,) + block.shape), axis)


def split3(v):
    hi = lax.reduce_precision(v, 8, 7)
    mid = lax.reduce_precision(v - hi, 8, 7)
    return jnp.stack([hi, mid, v - hi - mid]).astype(bf16)


def with_logs(block, logs):
    parts = split3(logs)
    rows = block.shape[0]
    tail = jnp.pad(parts, ((0, rows - 3), (0, EXTRA - logs.shape[0])))
    return jnp.concatenate([block, tail], axis=1)


def logs_of(blocks, width, heads):
    return blocks[:, 0:3, width : width + heads].astype(f32).sum(1)


def per_device(
    hidden_states,
    select_weight,
    conv_taps,
    inner_input,
    gate_input,
    step_size,
    decay_rate,
    skip_gain,
    tenant_scale,
    tenant_index,
    norm_gain,
):
    heads = decay_rate.shape[0]
    width = inner_input.shape[1]
    head_width = width // heads
    x, zh, zl = (lax.axis_index(a) for a in CTX)
    n_ctx = lax.axis_size(CTX)
    quad = lax.axis_size("zl")
    n_part = N // quad

    def lanes(v):
        return jnp.repeat(v, head_width, axis=-1)

    halo = lax.ppermute(hidden_states[Q - HALO :], CTX, [(i, i + 1) for i in range(n_ctx - 1)])
    rows_q = lax.all_gather(
        jnp.concatenate([halo, hidden_states], axis=0), "zl", axis=0, tiled=True
    )

    w_t = select_weight.T
    w_zh = share(w_t, "zh").reshape(-1, w_t.shape[1])
    w_all = share(w_zh, "x").reshape(-1, w_t.shape[1])

    seg_scale = lax.dynamic_index_in_dim(tenant_scale, tenant_index[0], 0, True).astype(f32)
    scaled = inner_input.astype(f32) * seg_scale
    driven = (scaled * lanes(step_size)).astype(bf16)
    cum = jnp.cumsum(-step_size * decay_rate[None, :], axis=0)
    weighted = (lanes(jnp.exp(cum[-1:] - cum)) * driven.astype(f32)).astype(bf16)
    weighted_q = lax.all_gather(with_logs(weighted, cum[-1]), "zl")

    part = lax.dot_general(
        w_all, rows_q, (((1,), (1,)), ((), ())), preferred_element_type=f32
    ).astype(bf16)
    raw = swap(part.reshape(lax.axis_size(TP), 2 * n_part, -1), TP).astype(f32).sum(0)
    taps = conv_taps.shape[0]
    own_taps = lax.dynamic_index_in_dim(
        conv_taps.reshape(taps, 2, quad, n_part), zl, 2, False
    ).reshape(taps, 2 * n_part)
    raw = raw.reshape(2 * n_part, quad, Q + HALO)
    summed = 0.0
    for k in range(taps):
        at = HALO - (taps - 1) + k
        summed = summed + own_taps[k][:, None, None] * raw[:, :, at : at + Q]
    keys = jnp.transpose(jax.nn.silu(summed).astype(bf16), (1, 0, 2))
    write_t, read_t = keys[:, :n_part], keys[:, n_part:]

    update = jnp.einsum(
        "bns,bsq->bnq", write_t, weighted_q[:, :, :width], preferred_element_type=f32
    )
    ends = logs_of(weighted_q, width, heads)
    state = jnp.zeros_like(update[0])
    starts = []
    for b in range(quad):
        starts.append(state)
        state = lanes(jnp.exp(ends[b]))[None] * state + update[b]

    def entering(total, logs, axis, place):
        got = share(with_logs(total.astype(bf16), logs), axis)
        got_logs = logs_of(got, width, heads)
        got = got[:, :, :width].astype(f32)
        acc, kept, all_acc = jnp.zeros_like(total), jnp.zeros_like(total), None
        log_kept = jnp.zeros_like(logs)
        log_acc = jnp.zeros_like(logs)
        for i in range(lax.axis_size(axis)):
            kept = jnp.where(place == i, acc, kept)
            log_kept = jnp.where(place == i, log_acc, log_kept)
            acc = lanes(jnp.exp(got_logs[i]))[None] * acc + got[i]
            log_acc = log_acc + got_logs[i]
        return kept, log_kept, acc, log_acc

    before, log_before, row, log_row = entering(state, ends.sum(0), "zh", zh)
    carry, _, _, _ = entering(row, log_row, "x", x)
    carry = lanes(jnp.exp(log_before))[None] * carry + before
    sent = []
    log_now = jnp.zeros_like(log_before)
    for b in range(quad):
        now = (starts[b] + lanes(jnp.exp(log_now))[None] * carry).astype(bf16)
        log_now = log_now + ends[b]
        sent.append(jnp.concatenate([now, write_t[b], read_t[b]], axis=1))
    own = swap(jnp.stack(sent), "zl").reshape(N, width + 2 * Q)
    start, write_t, read_t = own[:, :width], own[:, width : width + Q], own[:, width + Q :]

    scores = lax.dot_general(
        read_t, write_t, (((0,), (0,)), ((), ())), preferred_element_type=f32
    )
    cum_t = cum.T
    lag = cum_t[:, :, None] - cum_t[:, None, :]
    causal = jnp.tril(jnp.ones((Q, Q), dtype=bool))
    weights = jnp.where(causal, scores[None] * jnp.exp(jnp.where(causal, lag, 0.0)), 0.0).astype(bf16)
    within = jnp.einsum(
        "hts,shp->thp", weights, driven.reshape(Q, heads, head_width), preferred_element_type=f32
    ).reshape(Q, width)
    carried = lanes(jnp.exp(cum)) * lax.dot_general(
        read_t, start, (((0,), (0,)), ((), ())), preferred_element_type=f32
    )
    mixture = within + carried + lanes(skip_gain)[None] * scaled
    gated = mixture * jax.nn.silu(gate_input.astype(f32))
    meansq = jnp.mean(gated * gated, axis=-1, keepdims=True)
    normed = gated * lax.rsqrt(meansq + epsilon) * norm_gain.astype(f32)[None]
    return normed.astype(bf16)


def solution(mesh):
    fine = Mesh(mesh.devices.reshape(4, 4, 4, 4, 2), CTX + TP)
    in_specs = (
        P(CTX, TP),
        P(TP, CTX),
        P(None, TP),
        P(CTX, TP),
        P(CTX, TP),
        P(CTX, TP),
        P(TP),
        P(TP),
        P(None, TP),
        P(CTX),
        P(TP),
    )
    return jax.shard_map(
        per_device, mesh=fine, in_specs=in_specs, out_specs=P(CTX, TP), check_vma=False
    )
```

```python
import functools

import jax
import jax.numpy as jnp
from jax import lax
from jax.experimental import pallas as pl
from jax.experimental.pallas import tpu as pltpu
from jax.sharding import Mesh, PartitionSpec as P

N = 128
Q = 128
QUAD = 4
HALO = 16
LOG_ROWS = 16
CTX = ("x", "zh", "zl")
TP = ("y", "core")

epsilon = 1e-05
bf16 = jnp.bfloat16
f32 = jnp.float32
EXACT = lax.Precision.HIGHEST

VMEM = pl.BlockSpec(memory_space=pltpu.VMEM)
SMEM = pl.BlockSpec(memory_space=pltpu.SMEM)


def swap(blocks, axis):
    return lax.all_to_all(blocks, axis, 0, 0, tiled=True)


def share(block, axis):
    peers = lax.axis_size(axis)
    return swap(jnp.broadcast_to(block[None], (peers,) + block.shape), axis)


def shape(dims, kind):
    return jax.ShapeDtypeStruct(dims, kind)


def kernel_call(body, outs, place, args, scratch=(), flops=1_000_000):
    return pl.pallas_call(
        body,
        out_shape=outs,
        in_specs=[SMEM] + [VMEM] * len(args),
        out_specs=jax.tree.map(lambda _: VMEM, outs),
        scratch_shapes=scratch,
        compiler_params=pltpu.CompilerParams(vmem_limit_bytes=32 * 1024 * 1024),
        cost_estimate=pl.CostEstimate(flops=flops, bytes_accessed=1_000_000, transcendentals=0),
    )(place, *args)


def expand(columns, head_width):
    heads = columns.shape[1]
    shape2 = (heads, heads * head_width)
    head = lax.broadcasted_iota(jnp.int32, shape2, 0)
    lane = lax.broadcasted_iota(jnp.int32, shape2, 1)
    first = head * head_width
    onehot = jnp.where((lane >= first) & (lane < first + head_width), 1.0, 0.0)
    return jnp.dot(columns, onehot, precision=EXACT, preferred_element_type=f32)


def log_rows(row):
    hi = row.astype(bf16).astype(f32)
    mid = (row - hi).astype(bf16).astype(f32)
    low = row - hi - mid
    at = lax.broadcasted_iota(jnp.int32, (LOG_ROWS, row.shape[1]), 0)
    rows = jnp.where(at == 0, hi, jnp.where(at == 1, mid, jnp.where(at == 2, low, 0.0)))
    return rows.astype(bf16)


def log_row(rows):
    return jnp.sum(rows.astype(f32), axis=0, keepdims=True)


def scaled_by_tenant(tenant, inner_ref, scale_ref):
    row = lax.broadcasted_iota(jnp.int32, scale_ref.shape, 0)
    chosen = jnp.where(row == tenant, scale_ref[...].astype(f32), 0.0)
    return inner_ref[...].astype(f32) * jnp.sum(chosen, axis=0, keepdims=True)


def drive_kernel(
    place, inner, scale, step, decay, halo, driven, cum, cum_t, p0, p1, p2, p3, ext
):
    zl, tenant = place[2], place[3]
    width = inner.shape[1]
    head_width = width // step.shape[1]
    part_width = width // QUAD
    logs = -step[...] * decay[...]
    rows = lax.broadcasted_iota(jnp.int32, (Q, Q), 0)
    cols = lax.broadcasted_iota(jnp.int32, (Q, Q), 1)
    lower = jnp.where(rows >= cols, 1.0, 0.0)
    so_far = jnp.dot(lower, logs, precision=EXACT, preferred_element_type=f32)
    cum[...] = so_far
    cum_t[...] = lax.dot_general(
        logs, lower, (((0,), (1,)), ((), ())), precision=EXACT, preferred_element_type=f32
    )
    end = so_far[Q - 1 :]
    drive = (scaled_by_tenant(tenant, inner, scale) * expand(step[...], head_width)).astype(bf16)
    driven[...] = drive
    tail = expand(jnp.exp(end - so_far), head_width)
    ext[:Q] = (tail * drive.astype(f32)).astype(bf16)
    ext[Q : Q + LOG_ROWS] = log_rows(expand(end, head_width))
    ext[Q + LOG_ROWS :] = halo[...]
    for s, part in enumerate((p0, p1, p2, p3)):
        to = lax.rem(zl + s, QUAD)
        part[: Q + LOG_ROWS] = ext[
            : Q + LOG_ROWS, pl.ds(pl.multiple_of(to * part_width, part_width), part_width)
        ]
        for q in range(QUAD):
            at = Q + LOG_ROWS + q * HALO
            part[at : at + HALO] = ext[
                Q + LOG_ROWS :, q * part_width : (q + 1) * part_width
            ]


def project_kernel(place, w, h0, h1, h2, h3, p0, p1, p2, p3, out, halo):
    zl = place[2]
    at = Q + LOG_ROWS
    rows = [p[at:] for p in (p0, p1, p2, p3)]
    mine = rows[3]
    for s in range(QUAD - 1):
        mine = jnp.where(zl == s, rows[s], mine)
    part_width = mine.shape[1]
    halo[...] = jnp.zeros_like(halo)
    for q in range(QUAD):
        halo[Q - HALO :, q * part_width : (q + 1) * part_width] = mine[q * HALO : (q + 1) * HALO]
    for s, h in enumerate((h0, h1, h2, h3, halo)):
        out[:, s * Q : (s + 1) * Q] = lax.dot_general(
            w[...], h[...], (((1,), (1,)), ((), ())), preferred_element_type=f32
        ).astype(bf16)


def keys_kernel(place, parts, taps, out, selected):
    zl = place[2]
    raw = parts[0].astype(f32)
    for i in range(1, parts.shape[0]):
        raw = raw + parts[i].astype(f32)
    blocks = [raw[:, s * Q : (s + 1) * Q] for s in range(QUAD + 1)]
    lane = lax.broadcasted_iota(jnp.int32, blocks[0].shape, 1)
    n_taps = taps.shape[1]
    for s in range(QUAD):
        before = jnp.where(zl == s, blocks[QUAD], blocks[(s + 1) % QUAD])
        summed = taps[:, n_taps - 1 :] * blocks[s]
        for d in range(1, n_taps):
            moved = jnp.where(
                lane < d, pltpu.roll(before, d, 1), pltpu.roll(blocks[s], d, 1)
            )
            summed = summed + taps[:, n_taps - 1 - d : n_taps - d] * moved
        selected[:, s * Q : (s + 1) * Q] = (summed / (1.0 + jnp.exp(-summed))).astype(bf16)
    n_part = out.shape[1]
    for b in range(QUAD):
        s = lax.rem(zl - b + QUAD, QUAD)
        block = selected[:, pl.ds(pl.multiple_of(s * Q, Q), Q)]
        for to in range(QUAD):
            out[to, :, b * Q : (b + 1) * Q] = block[:n_part]
        out[b, :, QUAD * Q :] = block[n_part:]


def update_kernel(place, keys, p0, p1, p2, p3, starts, ends, total, update, logs):
    zl = place[2]
    for s, part in enumerate((p0, p1, p2, p3)):
        b = lax.rem(zl - s + QUAD, QUAD)
        block = keys[:, pl.ds(pl.multiple_of(b * Q, Q), Q)]
        update[b] = jnp.dot(block, part[:Q], preferred_element_type=f32)
        logs[b] = jnp.broadcast_to(log_row(part[Q : Q + LOG_ROWS]), logs.shape[1:])
    state = jnp.zeros(update.shape[1:], f32)
    all_logs = jnp.zeros((1, update.shape[2]), f32)
    for b in range(QUAD):
        starts[b] = state
        log = logs[b][:1]
        ends[b : b + 1] = log
        state = jnp.exp(log) * state + update[b]
        all_logs = all_logs + log
    total[:N] = state.astype(bf16)
    total[N:] = log_rows(all_logs)


def entering(got, place):
    acc = kept = jnp.zeros((N, got.shape[2]), f32)
    log_acc = log_kept = jnp.zeros((1, got.shape[2]), f32)
    for i in range(got.shape[0]):
        kept = jnp.where(place == i, acc, kept)
        log_kept = jnp.where(place == i, log_acc, log_kept)
        log = log_row(got[i, N:])
        acc = jnp.exp(log) * acc + got[i, :N].astype(f32)
        log_acc = log_acc + log
    return kept, log_kept, acc, log_acc


def row_kernel(place, got, before, log_before, total):
    kept, log_kept, acc, log_acc = entering(got, place[1])
    before[...] = kept
    log_before[...] = log_kept
    acc, log_acc = acc.astype(bf16), log_rows(log_acc)
    for i in range(total.shape[0]):
        total[i, :N] = acc
        total[i, N:] = log_acc


def states_kernel(place, got, before, log_before, starts, ends, out):
    carry = entering(got, place[0])[0]
    carry = jnp.exp(log_before[...]) * carry + before[...]
    log_now = jnp.zeros_like(log_before[...])
    for b in range(QUAD):
        out[b] = (starts[b] + jnp.exp(log_now) * carry).astype(bf16)
        log_now = log_now + ends[b : b + 1]


def within_kernel(place, keys, driven, cum, cum_t, inner, scale, skip, out):
    zl, tenant = place[2], place[3]
    read_t = keys[:, QUAD * Q :]
    write_t = keys[:, pl.ds(pl.multiple_of(zl * Q, Q), Q)]
    scores = lax.dot_general(
        read_t, write_t, (((0,), (0,)), ((), ())), preferred_element_type=f32
    )
    rows = lax.broadcasted_iota(jnp.int32, (Q, Q), 0)
    cols = lax.broadcasted_iota(jnp.int32, (Q, Q), 1)
    causal = rows >= cols
    heads = cum.shape[1]
    head_width = driven.shape[1] // heads
    per_tile = Q // head_width
    skipped = expand(skip[...], head_width) * scaled_by_tenant(tenant, inner, scale)
    for tile in range(heads // per_tile):
        at = slice(tile * Q, (tile + 1) * Q)
        mixed = None
        for i in range(per_tile):
            h = tile * per_tile + i
            lag = cum[:, h : h + 1] - cum_t[h : h + 1]
            weights = jnp.where(causal, scores * jnp.exp(jnp.where(causal, lag, 0.0)), 0.0)
            summed = jnp.dot(weights.astype(bf16), driven[:, at], preferred_element_type=f32)
            mixed = summed if mixed is None else jnp.where(cols < i * head_width, mixed, summed)
        out[:, at] = mixed + skipped[:, at]


def output_kernel(place, keys, start, cum, mixed, gate, gain, out):
    read_t = keys[:, QUAD * Q :]
    head_width = out.shape[1] // cum.shape[1]
    grown = expand(jnp.exp(cum[...]), head_width)
    part_width = start.shape[2]
    gated = []
    squares = jnp.zeros((Q, 1), f32)
    for q in range(QUAD):
        at = slice(q * part_width, (q + 1) * part_width)
        carried = lax.dot_general(
            read_t, start[q], (((0,), (0,)), ((), ())), preferred_element_type=f32
        )
        g = gate[:, at].astype(f32)
        value = (mixed[:, at] + grown[:, at] * carried) * (g / (1.0 + jnp.exp(-g)))
        squares = squares + jnp.sum(value * value, axis=1, keepdims=True)
        gated.append(value)
    inverse = lax.rsqrt(squares / out.shape[1] + epsilon)
    for q in range(QUAD):
        at = slice(q * part_width, (q + 1) * part_width)
        out[:, at] = (gated[q] * inverse * gain[:, at].astype(f32)).astype(bf16)


def per_device(
    hidden_states,
    select_weight,
    conv_taps,
    inner_input,
    gate_input,
    step_size,
    decay_rate,
    skip_gain,
    tenant_scale,
    tenant_index,
    norm_gain,
):
    heads = decay_rate.shape[0]
    width = inner_input.shape[1]
    x, zh, zl = (lax.axis_index(a) for a in CTX)
    place = jnp.stack([x, zh, zl, tenant_index[0]])
    n_ctx = lax.axis_size(CTX)
    n_part = N // QUAD
    part_width = width // QUAD
    part_rows = Q + LOG_ROWS + QUAD * HALO

    def by(s):
        return [(i, (i + s) % QUAD) for i in range(QUAD)]

    w_t = select_weight.T
    w_zh = lax.all_gather(w_t, "zh", axis=0, tiled=True)

    near = [lax.ppermute(hidden_states, "zl", by(s)) for s in (1, QUAD - 1)]
    halo = lax.ppermute(
        hidden_states[Q - HALO :], CTX, [(i, i + 1) for i in range(n_ctx - 1)]
    )
    w_zh, near, halo = lax.optimization_barrier((w_zh, near, halo))
    w_all = share(w_zh, "x").reshape(-1, w_t.shape[1])
    far = lax.ppermute(hidden_states, "zl", by(2))

    part = shape((part_rows, part_width), bf16)
    driven, cum, cum_t, *parts = kernel_call(
        drive_kernel,
        [shape((Q, width), bf16), shape((Q, heads), f32), shape((heads, Q), f32)] + [part] * QUAD,
        place,
        [inner_input, tenant_scale, step_size, decay_rate[None], halo],
        [pltpu.VMEM((Q + LOG_ROWS + HALO, width), bf16)],
    )
    parts[1:] = [lax.ppermute(parts[s], "zl", by(s)) for s in range(1, QUAD)]

    sums = kernel_call(
        project_kernel,
        shape((w_all.shape[0], (QUAD + 1) * Q), bf16),
        place,
        [w_all, hidden_states, near[0], far, near[1], *parts],
        [pltpu.VMEM((Q, w_all.shape[1]), bf16)],
    )
    raw = swap(sums.reshape(lax.axis_size(TP), 2 * n_part, -1), TP)
    taps = conv_taps.shape[0]
    own_taps = lax.dynamic_index_in_dim(
        conv_taps.reshape(taps, 2, QUAD, n_part), zl, 2, False
    ).reshape(taps, 2 * n_part)
    keys = kernel_call(
        keys_kernel,
        shape((QUAD, n_part, (QUAD + 1) * Q), bf16),
        place,
        [raw, own_taps.T],
        [pltpu.VMEM((2 * n_part, QUAD * Q), bf16)],
    )
    keys = swap(keys, "zl").reshape(N, -1)

    starts, ends, total = kernel_call(
        update_kernel,
        [
            shape((QUAD, N, part_width), f32),
            shape((QUAD, part_width), f32),
            shape((N + LOG_ROWS, part_width), bf16),
        ],
        place,
        [keys, *parts],
        [pltpu.VMEM((QUAD, N, part_width), f32), pltpu.VMEM((QUAD, 8, part_width), f32)],
    )
    got = lax.all_gather(total, "zh")
    before, log_before, row = kernel_call(
        row_kernel,
        [
            shape((N, part_width), f32),
            shape((1, part_width), f32),
            shape((lax.axis_size("x"), N + LOG_ROWS, part_width), bf16),
        ],
        place,
        [got],
    )
    states = kernel_call(
        states_kernel,
        shape((QUAD, N, part_width), bf16),
        place,
        [swap(row, "x"), before, log_before, starts, ends],
    )
    start = swap(states, "zl")

    mixed = kernel_call(
        within_kernel,
        shape((Q, width), f32),
        place,
        [keys, driven, cum, cum_t, inner_input, tenant_scale, skip_gain[None]],
    )
    return kernel_call(
        output_kernel,
        shape((Q, width), bf16),
        place,
        [keys, start, cum, mixed, gate_input, norm_gain[None]],
    )


def solution(mesh):
    fine = Mesh(mesh.devices.reshape(4, 4, 4, 4, 2), CTX + TP)
    in_specs = (
        P(CTX, TP),
        P(TP, CTX),
        P(None, TP),
        P(CTX, TP),
        P(CTX, TP),
        P(CTX, TP),
        P(TP),
        P(TP),
        P(None, TP),
        P(CTX),
        P(TP),
    )
    return jax.shard_map(
        per_device, mesh=fine, in_specs=in_specs, out_specs=P(CTX, TP), check_vma=False
    )
```

```python
import jax
import jax.numpy as jnp
from jax import lax
from jax.experimental import pallas as pl
from jax.experimental.pallas import tpu as pltpu
from jax.sharding import Mesh, PartitionSpec as P

N = 128
Q = 128
QUAD = 4
W_STEPS = (0, 2, -1, 1)
HALO = 16
LOG_ROWS = 16
Z = ("zh", "zl")
CTX = ("x",) + Z
NEAR = ("x", "zl")
TP = ("y", "core")

epsilon = 1e-05
bf16 = jnp.bfloat16
f32 = jnp.float32
EXACT = lax.Precision.HIGHEST

VMEM = pl.BlockSpec(memory_space=pltpu.VMEM)
SMEM = pl.BlockSpec(memory_space=pltpu.SMEM)


def swap(blocks, axis):
    return lax.all_to_all(blocks, axis, 0, 0, tiled=True)


def share(block, axis):
    peers = lax.axis_size(axis)
    return swap(jnp.broadcast_to(block[None], (peers,) + block.shape), axis)


def transpose_xy(block):
    side = lax.axis_size("x")
    pairs = [(i * side + j, j * side + i) for i in range(side) for j in range(side)]
    return lax.ppermute(block, ("x", "y"), pairs)


def shape(dims, kind):
    return jax.ShapeDtypeStruct(dims, kind)


def kernel_call(body, outs, place, args, scratch=(), flops=1_000_000):
    return pl.pallas_call(
        body,
        out_shape=outs,
        in_specs=[SMEM] + [VMEM] * len(args),
        out_specs=jax.tree.map(lambda _: VMEM, outs),
        scratch_shapes=scratch,
        compiler_params=pltpu.CompilerParams(vmem_limit_bytes=32 * 1024 * 1024),
        cost_estimate=pl.CostEstimate(flops=flops, bytes_accessed=1_000_000, transcendentals=0),
    )(place, *args)


def expand(columns, head_width):
    heads = columns.shape[1]
    shape2 = (heads, heads * head_width)
    head = lax.broadcasted_iota(jnp.int32, shape2, 0)
    lane = lax.broadcasted_iota(jnp.int32, shape2, 1)
    first = head * head_width
    onehot = jnp.where((lane >= first) & (lane < first + head_width), 1.0, 0.0)
    return jnp.dot(columns, onehot, precision=EXACT, preferred_element_type=f32)


def log_rows(row):
    hi = row.astype(bf16).astype(f32)
    mid = (row - hi).astype(bf16).astype(f32)
    low = row - hi - mid
    at = lax.broadcasted_iota(jnp.int32, (LOG_ROWS, row.shape[1]), 0)
    rows = jnp.where(at == 0, hi, jnp.where(at == 1, mid, jnp.where(at == 2, low, 0.0)))
    return rows.astype(bf16)


def log_row(rows):
    return jnp.sum(rows.astype(f32), axis=0, keepdims=True)


def scaled_by_tenant(tenant, inner_ref, scale_ref):
    row = lax.broadcasted_iota(jnp.int32, scale_ref.shape, 0)
    chosen = jnp.where(row == tenant, scale_ref[...].astype(f32), 0.0)
    return inner_ref[...].astype(f32) * jnp.sum(chosen, axis=0, keepdims=True)


def drive_kernel(place, inner, scale, step, decay, driven, cum, cum_t, weighted_t, logs):
    heads = step.shape[1]
    head_width = inner.shape[1] // heads
    log_decay = -step[...] * decay[...]
    rows = lax.broadcasted_iota(jnp.int32, (Q, Q), 0)
    cols = lax.broadcasted_iota(jnp.int32, (Q, Q), 1)
    lower = jnp.where(rows >= cols, 1.0, 0.0)
    so_far = jnp.dot(lower, log_decay, precision=EXACT, preferred_element_type=f32)
    cum[...] = so_far
    cum_t[...] = lax.dot_general(
        log_decay, lower, (((0,), (1,)), ((), ())), precision=EXACT, preferred_element_type=f32
    )
    end = so_far[Q - 1 :]
    scaled = scaled_by_tenant(place[3], inner, scale)
    drive = (scaled * expand(step[...], head_width)).astype(bf16)
    driven[...] = drive
    tail = expand(jnp.exp(end - so_far), head_width)
    weighted_t[...] = jnp.transpose(tail * drive.astype(f32)).astype(bf16)
    for h in range(heads):
        logs[h] = log_rows(jnp.broadcast_to(end[:, h : h + 1], (1, N)))


def share_kernel(place, block, out):
    for i in range(out.shape[0]):
        out[i] = block[...]


def project_kernel(place, w0, w1, w2, w3, rows, tails, out, w_in_order, all_rows):
    halves, n_part = w0.shape[:2]
    for w, step in zip((w0, w1, w2, w3), W_STEPS):
        s = lax.rem(place[2] + step + QUAD, QUAD)
        for i in range(halves):
            at = pl.multiple_of(i * N + s * n_part, n_part)
            w_in_order[pl.ds(at, n_part)] = w[i]
    first = (place[1] == 0) & (place[2] == 0)
    size = HALO + Q
    for block in range(rows.shape[0]):
        behind = tails[block - 1] if block > 0 else jnp.zeros_like(tails[0])
        all_rows[block * size : block * size + HALO] = jnp.where(first, behind, tails[block])
        all_rows[block * size + HALO : (block + 1) * size] = rows[block]
    for c in range(out.shape[1]):
        sums = lax.dot_general(
            all_rows[...],
            w_in_order[c * 2 * N : (c + 1) * 2 * N],
            (((1,), (1,)), ((), ())),
            preferred_element_type=f32,
        ).astype(bf16)
        for block in range(rows.shape[0]):
            out[block, c] = sums[block * size : (block + 1) * size]


def sum_kernel(place, parts, out):
    raw = parts[0].astype(f32)
    for i in range(1, parts.shape[0]):
        raw = raw + parts[i].astype(f32)
    out[...] = raw.astype(bf16)


def keys_kernel(place, sums, taps, weighted_t, logs, keys_out, out):
    raw = sums[...].astype(f32)
    n_taps = taps.shape[0]
    summed = taps[n_taps - 1 :] * raw[HALO:]
    for d in range(1, n_taps):
        summed = summed + taps[n_taps - 1 - d : n_taps - d] * raw[HALO - d : HALO - d + Q]
    keys = (summed / (1.0 + jnp.exp(-summed))).astype(bf16)
    keys_out[...] = keys
    update = jnp.dot(weighted_t[...], keys[:, :N], preferred_element_type=f32).astype(bf16)
    heads = out.shape[0]
    head_width = update.shape[0] // heads
    for h in range(heads):
        out[h, :head_width] = update[h * head_width : (h + 1) * head_width]
        out[h, head_width:] = logs[h]


def total_kernel(place, got, total):
    head_width = got.shape[1] - LOG_ROWS
    for row in range(total.shape[0]):
        acc = jnp.zeros((head_width, N), f32)
        log_acc = jnp.zeros((1, N), f32)
        for b in range(QUAD):
            log = log_row(got[row * QUAD + b, head_width:])
            acc = jnp.exp(log) * acc + got[row * QUAD + b, :head_width].astype(f32)
            log_acc = log_acc + log
        total[row, :head_width] = acc.astype(bf16)
        total[row, head_width:] = log_rows(log_acc)


def states_kernel(place, totals, got, out):
    head_width = out.shape[1]
    acc = jnp.zeros((head_width, N), f32)
    for row in range(totals.shape[1]):
        carry = acc
        for quad in range(totals.shape[0]):
            carry = jnp.where(place[1] == quad, acc, carry)
            log = log_row(totals[quad, row, head_width:])
            acc = jnp.exp(log) * acc + totals[quad, row, :head_width].astype(f32)
        for b in range(QUAD):
            at = row * QUAD + b
            out[at] = carry.astype(bf16)
            if b < QUAD - 1:
                log = log_row(got[at, head_width:])
                carry = jnp.exp(log) * carry + got[at, :head_width].astype(f32)


def within_kernel(place, keys, driven, cum, cum_t, inner, scale, skip, gate, out, grown):
    scores = lax.dot_general(
        keys[:, N:], keys[:, :N], (((1,), (1,)), ((), ())), preferred_element_type=f32
    )
    rows = lax.broadcasted_iota(jnp.int32, (Q, Q), 0)
    cols = lax.broadcasted_iota(jnp.int32, (Q, Q), 1)
    causal = rows >= cols
    heads = cum.shape[1]
    head_width = driven.shape[1] // heads
    per_tile = Q // head_width
    skipped = expand(skip[...], head_width) * scaled_by_tenant(place[3], inner, scale)
    g = gate[...].astype(f32)
    gates = g / (1.0 + jnp.exp(-g))
    grown[...] = gates * expand(jnp.exp(cum[...]), head_width)
    for tile in range(heads // per_tile):
        at = slice(tile * Q, (tile + 1) * Q)
        mixed = None
        for i in range(per_tile):
            h = tile * per_tile + i
            lag = cum[:, h : h + 1] - cum_t[h : h + 1]
            weights = jnp.where(causal, scores * jnp.exp(jnp.where(causal, lag, 0.0)), 0.0)
            summed = jnp.dot(weights.astype(bf16), driven[:, at], preferred_element_type=f32)
            mixed = summed if mixed is None else jnp.where(cols < i * head_width, mixed, summed)
        out[:, at] = (mixed + skipped[:, at]) * gates[:, at]


def output_kernel(place, keys, start, mixed, grown, gain, out):
    width = out.shape[1]
    quarter = width // QUAD
    gated = []
    squares = jnp.zeros((Q, 1), f32)
    for q in range(QUAD):
        at = slice(q * quarter, (q + 1) * quarter)
        carried = lax.dot_general(
            keys[:, N:], start[at], (((1,), (1,)), ((), ())), preferred_element_type=f32
        )
        value = mixed[:, at] + grown[:, at] * carried
        squares = squares + jnp.sum(value * value, axis=1, keepdims=True)
        gated.append(value)
    inverse = lax.rsqrt(squares / width + epsilon)
    for q in range(QUAD):
        at = slice(q * quarter, (q + 1) * quarter)
        out[:, at] = (gated[q] * inverse * gain[:, at].astype(f32)).astype(bf16)


def per_device(
    hidden_states,
    select_weight,
    conv_taps,
    inner_input,
    gate_input,
    step_size,
    decay_rate,
    skip_gain,
    tenant_scale,
    tenant_index,
    norm_gain,
):
    heads = decay_rate.shape[0]
    width = inner_input.shape[1]
    head_width = width // heads
    x, zh, zl = (lax.axis_index(a) for a in CTX)
    place = jnp.stack([x, zh, zl, tenant_index[0]])
    n_z = lax.axis_size(Z)
    n_x = lax.axis_size("x")
    depth = hidden_states.shape[1]

    rows = swap(
        kernel_call(
            share_kernel, shape((n_x,) + hidden_states.shape, bf16), place, [hidden_states]
        ),
        "x",
    )

    n_part = select_weight.shape[1]
    w_zh = lax.all_gather(select_weight.T, "zh")
    w_zh, rows = lax.optimization_barrier((w_zh, rows))
    w_all = [w_zh] + [
        lax.ppermute(w_zh, Z, [(i, (i - step) % n_z) for i in range(n_z)]) for step in W_STEPS[1:]
    ]

    tails = lax.ppermute(rows[:, Q - HALO :], Z, [(i, (i + 1) % n_z) for i in range(n_z)])

    driven, cum, cum_t, weighted_t, logs = kernel_call(
        drive_kernel,
        [
            shape((Q, width), bf16),
            shape((Q, heads), f32),
            shape((heads, Q), f32),
            shape((width, Q), bf16),
            shape((heads, LOG_ROWS, N), bf16),
        ],
        place,
        [inner_input, tenant_scale, step_size, decay_rate[None]],
    )


    size = HALO + Q
    sums = kernel_call(
        project_kernel,
        shape((n_x, lax.axis_size("core"), size, 2 * N), bf16),
        place,
        [*w_all, rows, tails],
        [
            pltpu.VMEM((w_zh.shape[0] * QUAD * n_part, depth), bf16),
            pltpu.VMEM((n_x * size, depth), bf16),
        ],
    )
    sums = swap(sums.reshape(-1, size, 2 * N), TP)
    sums, weighted_t, logs = lax.optimization_barrier((sums, weighted_t, logs))
    sums = transpose_xy(kernel_call(sum_kernel, shape((size, 2 * N), bf16), place, [sums]))
    keys, update = kernel_call(
        keys_kernel,
        [shape((Q, 2 * N), bf16), shape((heads, head_width + LOG_ROWS, N), bf16)],
        place,
        [sums, conv_taps, weighted_t, logs],
    )

    got = swap(update, NEAR)
    total = kernel_call(
        total_kernel, shape((n_x, head_width + LOG_ROWS, N), bf16), place, [got]
    )
    states = kernel_call(
        states_kernel,
        shape((heads, head_width, N), bf16),
        place,
        [lax.all_gather(total, "zh"), got],
    )
    start = swap(states, NEAR).reshape(width, N)

    mixed, grown = kernel_call(
        within_kernel,
        [shape((Q, width), f32)] * 2,
        place,
        [keys, driven, cum, cum_t, inner_input, tenant_scale, skip_gain[None], gate_input],
    )
    return kernel_call(
        output_kernel,
        shape((Q, width), bf16),
        place,
        [keys, start, mixed, grown, norm_gain[None]],
    )


def solution(mesh):
    fine = Mesh(mesh.devices.reshape(4, 4, 4, 4, 2), CTX + TP)
    in_specs = (
        P(CTX, TP),
        P(TP, CTX),
        P(None, TP),
        P(CTX, TP),
        P(CTX, TP),
        P(CTX, TP),
        P(TP),
        P(TP),
        P(None, TP),
        P(CTX),
        P(TP),
    )
    return jax.shard_map(
        per_device, mesh=fine, in_specs=in_specs, out_specs=P(CTX, TP), check_vma=False
    )
```

```python
import jax
import jax.numpy as jnp
from jax import lax
from jax.experimental import pallas as pl
from jax.experimental.pallas import tpu as pltpu
from jax.sharding import Mesh, PartitionSpec as P

N = 128
Q = 128
QUAD = 4
W_STEPS = (0, 2, -1, 1)
HALO = 16
LOG_ROWS = 16
Z = ("zh", "zl")
CTX = ("x",) + Z
NEAR = ("x", "zl")
TP = ("y", "core")

epsilon = 1e-05
bf16 = jnp.bfloat16
f32 = jnp.float32
EXACT = lax.Precision.HIGHEST

VMEM = pl.BlockSpec(memory_space=pltpu.VMEM)
SMEM = pl.BlockSpec(memory_space=pltpu.SMEM)


def swap(blocks, axis):
    return lax.all_to_all(blocks, axis, 0, 0, tiled=True)


def share(block, axis):
    peers = lax.axis_size(axis)
    return swap(jnp.broadcast_to(block[None], (peers,) + block.shape), axis)


def to_owner(block):
    side = lax.axis_size("x")
    pairs = [
        (i * side + j, (j + side // 2) % side * side + i) for i in range(side) for j in range(side)
    ]
    return lax.ppermute(block, ("x", "y"), pairs)


def shape(dims, kind):
    return jax.ShapeDtypeStruct(dims, kind)


def kernel_call(body, outs, place, args, scratch=(), flops=1_000_000):
    return pl.pallas_call(
        body,
        out_shape=outs,
        in_specs=[SMEM] + [VMEM] * len(args),
        out_specs=jax.tree.map(lambda _: VMEM, outs),
        scratch_shapes=scratch,
        compiler_params=pltpu.CompilerParams(vmem_limit_bytes=32 * 1024 * 1024),
        cost_estimate=pl.CostEstimate(flops=flops, bytes_accessed=1_000_000, transcendentals=0),
    )(place, *args)


def expand(columns, head_width):
    heads = columns.shape[1]
    shape2 = (heads, heads * head_width)
    head = lax.broadcasted_iota(jnp.int32, shape2, 0)
    lane = lax.broadcasted_iota(jnp.int32, shape2, 1)
    first = head * head_width
    onehot = jnp.where((lane >= first) & (lane < first + head_width), 1.0, 0.0)
    return jnp.dot(columns, onehot, precision=EXACT, preferred_element_type=f32)


def split3(row):
    hi = row.astype(bf16).astype(f32)
    mid = (row - hi).astype(bf16).astype(f32)
    return hi, mid, row - hi - mid


def log_rows(row):
    hi, mid, low = split3(row)
    at = lax.broadcasted_iota(jnp.int32, (LOG_ROWS, row.shape[1]), 0)
    rows = jnp.where(at == 0, hi, jnp.where(at == 1, mid, jnp.where(at == 2, low, 0.0)))
    return rows.astype(bf16)


def log_row(rows):
    return jnp.sum(rows.astype(f32), axis=0, keepdims=True)


def scaled_by_tenant(tenant, inner_ref, scale_ref):
    row = lax.broadcasted_iota(jnp.int32, scale_ref.shape, 0)
    chosen = jnp.where(row == tenant, scale_ref[...].astype(f32), 0.0)
    return inner_ref[...].astype(f32) * jnp.sum(chosen, axis=0, keepdims=True)


def drive_kernel(place, inner, scale, step, decay, driven, cum, cum_t, weighted_t, logs):
    heads = step.shape[1]
    head_width = inner.shape[1] // heads
    log_decay = -step[...] * decay[...]
    rows = lax.broadcasted_iota(jnp.int32, (Q, Q), 0)
    cols = lax.broadcasted_iota(jnp.int32, (Q, Q), 1)
    lower = jnp.where(rows >= cols, 1.0, 0.0)
    so_far = jnp.dot(lower, log_decay, precision=EXACT, preferred_element_type=f32)
    cum[...] = so_far
    cum_t[...] = lax.dot_general(
        log_decay, lower, (((0,), (1,)), ((), ())), precision=EXACT, preferred_element_type=f32
    )
    end = so_far[Q - 1 :]
    scaled = scaled_by_tenant(place[3], inner, scale)
    drive = (scaled * expand(step[...], head_width)).astype(bf16)
    driven[...] = drive
    tail = expand(jnp.exp(end - so_far), head_width)
    weighted_t[...] = jnp.transpose(tail * drive.astype(f32)).astype(bf16)
    for h in range(heads):
        logs[h] = log_rows(jnp.broadcast_to(end[:, h : h + 1], (1, N)))


def share_kernel(block, out, held, arrived, sent):
    fetch = pltpu.make_async_copy(block, held, arrived)
    fetch.start()
    fetch.wait()
    copies = [pltpu.make_async_copy(held, out.at[i], sent.at[i]) for i in range(out.shape[0])]
    for copy in copies:
        copy.start()
    for copy in copies:
        copy.wait()


def project_kernel(place, w0, w1, w2, w3, rows, out, w_in_order, all_rows):
    n_part = N // QUAD
    halves = w0.shape[0] // n_part
    for w, step in zip((w0, w1, w2, w3), W_STEPS):
        s = lax.rem(place[2] + step + QUAD, QUAD)
        for i in range(halves):
            at = pl.multiple_of(i * N + s * n_part, n_part)
            w_in_order[pl.ds(at, n_part)] = w[i * n_part : (i + 1) * n_part]
    tails = [
        w2[halves * n_part + i * HALO : halves * n_part + (i + 1) * HALO]
        for i in range(rows.shape[0])
    ]
    first = (place[1] == 0) & (place[2] == 0)
    size = HALO + Q
    for block in range(rows.shape[0]):
        behind = tails[block - 1] if block > 0 else jnp.zeros_like(tails[0])
        all_rows[block * size : block * size + HALO] = jnp.where(first, behind, tails[block])
        all_rows[block * size + HALO : (block + 1) * size] = rows[block]
    for c in range(out.shape[1]):
        sums = lax.dot_general(
            all_rows[...],
            w_in_order[c * 2 * N : (c + 1) * 2 * N],
            (((1,), (1,)), ((), ())),
            preferred_element_type=f32,
        ).astype(bf16)
        for block in range(rows.shape[0]):
            to = (block + rows.shape[0] // 2) % rows.shape[0]
            out[to, c] = sums[block * size : (block + 1) * size]


def sum_kernel(place, parts, out):
    raw = parts[0].astype(f32)
    for i in range(1, parts.shape[0]):
        raw = raw + parts[i].astype(f32)
    out[...] = raw.astype(bf16)


def keys_kernel(place, sums, taps, weighted_t, logs, keys_out, out):
    raw = sums[...].astype(f32)
    n_taps = taps.shape[0]
    summed = taps[n_taps - 1 :] * raw[HALO:]
    for d in range(1, n_taps):
        summed = summed + taps[n_taps - 1 - d : n_taps - d] * raw[HALO - d : HALO - d + Q]
    keys = (summed / (1.0 + jnp.exp(-summed))).astype(bf16)
    keys_out[...] = keys
    update = jnp.dot(weighted_t[...], keys[:, :N], preferred_element_type=f32).astype(bf16)
    heads = out.shape[0]
    head_width = update.shape[0] // heads
    for h in range(heads):
        out[h, :head_width] = update[h * head_width : (h + 1) * head_width]
        out[h, head_width:] = logs[h]


def total_kernel(place, got, total):
    head_width = got.shape[1] - LOG_ROWS
    rows = got.shape[0] // QUAD
    at = lax.broadcasted_iota(jnp.int32, (LOG_ROWS, N), 0)
    logs = jnp.zeros((LOG_ROWS, N), f32)
    for row in range(rows):
        acc = jnp.zeros((head_width, N), f32)
        log_acc = jnp.zeros((1, N), f32)
        for b in range(QUAD):
            log = log_row(got[row * QUAD + b, head_width:])
            acc = jnp.exp(log) * acc + got[row * QUAD + b, :head_width].astype(f32)
            log_acc = log_acc + log
        total[row * head_width : (row + 1) * head_width] = acc.astype(bf16)
        for i, part in enumerate(split3(log_acc)):
            logs = jnp.where(at == row * 3 + i, part, logs)
    total[rows * head_width :] = logs.astype(bf16)


def states_kernel(place, totals, got, out):
    head_width = out.shape[1]
    rows = out.shape[0] // QUAD
    logs = [totals[quad, rows * head_width :].astype(f32) for quad in range(totals.shape[0])]
    acc = jnp.zeros((head_width, N), f32)
    for row in range(rows):
        carry = acc
        for quad in range(totals.shape[0]):
            carry = jnp.where(place[1] == quad, acc, carry)
            log = jnp.sum(logs[quad][3 * row : 3 * row + 3], axis=0, keepdims=True)
            update = totals[quad, row * head_width : (row + 1) * head_width]
            acc = jnp.exp(log) * acc + update.astype(f32)
        for b in range(QUAD):
            at = row * QUAD + b
            out[at] = carry.astype(bf16)
            if b < QUAD - 1:
                log = log_row(got[at, head_width:])
                carry = jnp.exp(log) * carry + got[at, :head_width].astype(f32)


def within_kernel(place, keys, driven, cum, cum_t, inner, scale, skip, gate, out, grown):
    scores = lax.dot_general(
        keys[:, N:], keys[:, :N], (((1,), (1,)), ((), ())), preferred_element_type=f32
    )
    rows = lax.broadcasted_iota(jnp.int32, (Q, Q), 0)
    cols = lax.broadcasted_iota(jnp.int32, (Q, Q), 1)
    causal = rows >= cols
    heads = cum.shape[1]
    head_width = driven.shape[1] // heads
    per_tile = Q // head_width
    skipped = expand(skip[...], head_width) * scaled_by_tenant(place[3], inner, scale)
    g = gate[...].astype(f32)
    gates = g / (1.0 + jnp.exp(-g))
    grown[...] = gates * expand(jnp.exp(cum[...]), head_width)
    for tile in range(heads // per_tile):
        at = slice(tile * Q, (tile + 1) * Q)
        mixed = None
        for i in range(per_tile):
            h = tile * per_tile + i
            lag = cum[:, h : h + 1] - cum_t[h : h + 1]
            weights = jnp.where(causal, scores * jnp.exp(jnp.where(causal, lag, 0.0)), 0.0)
            summed = jnp.dot(weights.astype(bf16), driven[:, at], preferred_element_type=f32)
            mixed = summed if mixed is None else jnp.where(cols < i * head_width, mixed, summed)
        out[:, at] = (mixed + skipped[:, at]) * gates[:, at]


def output_kernel(place, keys, start, mixed, grown, gain, out):
    width = out.shape[1]
    quarter = width // QUAD
    gated = []
    squares = jnp.zeros((Q, 1), f32)
    for q in range(QUAD):
        at = slice(q * quarter, (q + 1) * quarter)
        carried = lax.dot_general(
            keys[:, N:], start[at], (((1,), (1,)), ((), ())), preferred_element_type=f32
        )
        value = mixed[:, at] + grown[:, at] * carried
        squares = squares + jnp.sum(value * value, axis=1, keepdims=True)
        gated.append(value)
    inverse = lax.rsqrt(squares / width + epsilon)
    for q in range(QUAD):
        at = slice(q * quarter, (q + 1) * quarter)
        out[:, at] = (gated[q] * inverse * gain[:, at].astype(f32)).astype(bf16)


def per_device(
    hidden_states,
    select_weight,
    conv_taps,
    inner_input,
    gate_input,
    step_size,
    decay_rate,
    skip_gain,
    tenant_scale,
    tenant_index,
    norm_gain,
):
    heads = decay_rate.shape[0]
    width = inner_input.shape[1]
    head_width = width // heads
    x, zh, zl = (lax.axis_index(a) for a in CTX)
    place = jnp.stack([x, zh, zl, tenant_index[0]])
    n_z = lax.axis_size(Z)
    n_x = lax.axis_size("x")
    depth = hidden_states.shape[1]

    rows = pl.pallas_call(
        share_kernel,
        out_shape=shape((n_x,) + hidden_states.shape, bf16),
        in_specs=[pl.BlockSpec(memory_space=pl.ANY)],
        out_specs=pl.BlockSpec(memory_space=pl.ANY),
        scratch_shapes=[
            pltpu.VMEM(hidden_states.shape, bf16),
            pltpu.SemaphoreType.DMA,
            pltpu.SemaphoreType.DMA((n_x,)),
        ],
        cost_estimate=pl.CostEstimate(flops=0, bytes_accessed=1_000_000, transcendentals=0),
    )(hidden_states)
    rows = swap(rows, "x")

    n_part = select_weight.shape[1]
    w_zh = lax.all_gather(select_weight.T, "zh", axis=0, tiled=True)
    w_zh, rows = lax.optimization_barrier((w_zh, rows))
    n_core = lax.axis_size("core")
    tails = rows[:, Q - HALO :].reshape(n_x * HALO, depth)
    w_all = [w_zh] + [
        lax.ppermute(
            jnp.concatenate([w_zh, tails], axis=0) if step == -1 else w_zh,
            Z + ("core",),
            [
                (i * n_core + c, (i - step * (1 if c == 0 else turn)) % n_z * n_core + c)
                for i in range(n_z)
                for c in range(n_core)
            ],
        )
        for step, turn in zip(W_STEPS[1:], (-1, 1, 1))
    ]

    driven, cum, cum_t, weighted_t, logs = kernel_call(
        drive_kernel,
        [
            shape((Q, width), bf16),
            shape((Q, heads), f32),
            shape((heads, Q), f32),
            shape((width, Q), bf16),
            shape((heads, LOG_ROWS, N), bf16),
        ],
        place,
        [inner_input, tenant_scale, step_size, decay_rate[None]],
    )


    w_all, weighted_t, logs = lax.optimization_barrier((w_all, weighted_t, logs))

    size = HALO + Q
    sums = kernel_call(
        project_kernel,
        shape((n_x, lax.axis_size("core"), size, 2 * N), bf16),
        place,
        [*w_all, rows],
        [
            pltpu.VMEM((w_zh.shape[0] * QUAD, depth), bf16),
            pltpu.VMEM((n_x * size, depth), bf16),
        ],
    )
    sums = swap(sums.reshape(-1, size, 2 * N), TP)
    sums = to_owner(kernel_call(sum_kernel, shape((size, 2 * N), bf16), place, [sums]))
    keys, update = kernel_call(
        keys_kernel,
        [shape((Q, 2 * N), bf16), shape((heads, head_width + LOG_ROWS, N), bf16)],
        place,
        [sums, conv_taps, weighted_t, logs],
    )

    got = swap(update, NEAR)
    total = kernel_call(
        total_kernel, shape((n_x * head_width + LOG_ROWS, N), bf16), place, [got]
    )
    states = kernel_call(
        states_kernel,
        shape((heads, head_width, N), bf16),
        place,
        [lax.all_gather(total, "zh"), got],
    )
    start = swap(states, NEAR).reshape(width, N)

    mixed, grown = kernel_call(
        within_kernel,
        [shape((Q, width), f32)] * 2,
        place,
        [keys, driven, cum, cum_t, inner_input, tenant_scale, skip_gain[None], gate_input],
    )
    return kernel_call(
        output_kernel,
        shape((Q, width), bf16),
        place,
        [keys, start, mixed, grown, norm_gain[None]],
    )


def solution(mesh):
    fine = Mesh(mesh.devices.reshape(4, 4, 4, 4, 2), CTX + TP)
    in_specs = (
        P(CTX, TP),
        P(TP, CTX),
        P(None, TP),
        P(CTX, TP),
        P(CTX, TP),
        P(CTX, TP),
        P(TP),
        P(TP),
        P(None, TP),
        P(CTX),
        P(TP),
    )
    return jax.shard_map(
        per_device, mesh=fine, in_specs=in_specs, out_specs=P(CTX, TP), check_vma=False
    )
```

```python
import jax
import jax.numpy as jnp
from jax import lax
from jax.experimental import pallas as pl
from jax.experimental.pallas import tpu as pltpu
from jax.sharding import Mesh, PartitionSpec as P

N = 128
Q = 128
QUAD = 4
W_STEPS = (0, 1, -1, 2)
HALO = 16
REACH = 3
LOG_ROWS = 16
Z = ("zh", "zl")
CTX = ("x",) + Z
NEAR = ("x", "zl")
TP = ("y", "core")

epsilon = 1e-05
bf16 = jnp.bfloat16
f32 = jnp.float32
EXACT = lax.Precision.HIGHEST

VMEM = pl.BlockSpec(memory_space=pltpu.VMEM)
SMEM = pl.BlockSpec(memory_space=pltpu.SMEM)


def swap(blocks, axis):
    return lax.all_to_all(blocks, axis, 0, 0, tiled=True)


def share(block, axis):
    peers = lax.axis_size(axis)
    return swap(jnp.broadcast_to(block[None], (peers,) + block.shape), axis)


def to_owner(block):
    side = lax.axis_size("x")
    pairs = [
        (i * side + j, (j + side // 2) % side * side + i) for i in range(side) for j in range(side)
    ]
    return lax.ppermute(block, ("x", "y"), pairs)


def shape(dims, kind):
    return jax.ShapeDtypeStruct(dims, kind)


def kernel_call(body, outs, place, args, scratch=(), flops=1_000_000):
    return pl.pallas_call(
        body,
        out_shape=outs,
        in_specs=[SMEM] + [VMEM] * len(args),
        out_specs=jax.tree.map(lambda _: VMEM, outs),
        scratch_shapes=scratch,
        compiler_params=pltpu.CompilerParams(vmem_limit_bytes=32 * 1024 * 1024),
        cost_estimate=pl.CostEstimate(flops=flops, bytes_accessed=1_000_000, transcendentals=0),
    )(place, *args)


def expand(columns, head_width):
    heads = columns.shape[1]
    shape2 = (heads, heads * head_width)
    head = lax.broadcasted_iota(jnp.int32, shape2, 0)
    lane = lax.broadcasted_iota(jnp.int32, shape2, 1)
    first = head * head_width
    onehot = jnp.where((lane >= first) & (lane < first + head_width), 1.0, 0.0)
    return jnp.dot(columns, onehot, precision=EXACT, preferred_element_type=f32)


def split3(row):
    hi = row.astype(bf16).astype(f32)
    mid = (row - hi).astype(bf16).astype(f32)
    return hi, mid, row - hi - mid


def log_rows(row):
    hi, mid, low = split3(row)
    at = lax.broadcasted_iota(jnp.int32, (LOG_ROWS, row.shape[1]), 0)
    rows = jnp.where(at == 0, hi, jnp.where(at == 1, mid, jnp.where(at == 2, low, 0.0)))
    return rows.astype(bf16)


def log_row(rows):
    return jnp.sum(rows.astype(f32), axis=0, keepdims=True)


def scaled_by_tenant(tenant, inner_ref, scale_ref):
    row = lax.broadcasted_iota(jnp.int32, scale_ref.shape, 0)
    chosen = jnp.where(row == tenant, scale_ref[...].astype(f32), 0.0)
    return inner_ref[...].astype(f32) * jnp.sum(chosen, axis=0, keepdims=True)


def drive_kernel(place, inner, scale, step, decay, driven, cum, cum_t, weighted_t, logs):
    heads = step.shape[1]
    head_width = inner.shape[1] // heads
    log_decay = -step[...] * decay[...]
    rows = lax.broadcasted_iota(jnp.int32, (Q, Q), 0)
    cols = lax.broadcasted_iota(jnp.int32, (Q, Q), 1)
    lower = jnp.where(rows >= cols, 1.0, 0.0)
    so_far = jnp.dot(lower, log_decay, precision=EXACT, preferred_element_type=f32)
    cum[...] = so_far
    cum_t[...] = lax.dot_general(
        log_decay, lower, (((0,), (1,)), ((), ())), precision=EXACT, preferred_element_type=f32
    )
    end = so_far[Q - 1 :]
    scaled = scaled_by_tenant(place[3], inner, scale)
    drive = (scaled * expand(step[...], head_width)).astype(bf16)
    driven[...] = drive
    tail = expand(jnp.exp(end - so_far), head_width)
    weighted_t[...] = jnp.transpose(tail * drive.astype(f32)).astype(bf16)
    for h in range(heads):
        logs[h] = log_rows(jnp.broadcast_to(end[:, h : h + 1], (1, N)))


def share_kernel(block, out, held, arrived, sent):
    fetch = pltpu.make_async_copy(block, held, arrived)
    fetch.start()
    fetch.wait()
    copies = [pltpu.make_async_copy(held, out.at[i], sent.at[i]) for i in range(out.shape[0])]
    for copy in copies:
        copy.start()
    for copy in copies:
        copy.wait()


def project_kernel(place, w0, w1, w2, w3, rows, out, w_in_order, all_rows):
    n_part = N // QUAD
    halves = w0.shape[0] // n_part
    for w, step in zip((w0, w1, w2, w3), W_STEPS):
        s = lax.rem(place[2] + step + QUAD, QUAD)
        for i in range(halves):
            at = pl.multiple_of(i * N + s * n_part, n_part)
            w_in_order[pl.ds(at, n_part)] = w[i * n_part : (i + 1) * n_part]
    packed = w2[halves * n_part :].astype(f32)
    tails = [
        pltpu.roll(packed, (HALO - (i + 1) * REACH) % HALO, 0).astype(bf16)
        for i in range(rows.shape[0])
    ]
    first = (place[1] == 0) & (place[2] == 0)
    size = HALO + Q
    for block in range(rows.shape[0]):
        behind = tails[block - 1] if block > 0 else jnp.zeros_like(tails[0])
        all_rows[block * size : block * size + HALO] = jnp.where(first, behind, tails[block])
        all_rows[block * size + HALO : (block + 1) * size] = rows[block]
    for c in range(out.shape[1]):
        sums = lax.dot_general(
            all_rows[...],
            w_in_order[c * 2 * N : (c + 1) * 2 * N],
            (((1,), (1,)), ((), ())),
            preferred_element_type=f32,
        ).astype(bf16)
        for block in range(rows.shape[0]):
            to = (block + rows.shape[0] // 2) % rows.shape[0]
            out[to, c] = sums[block * size : (block + 1) * size]


def sum_kernel(place, parts, out):
    raw = parts[0].astype(f32)
    for i in range(1, parts.shape[0]):
        raw = raw + parts[i].astype(f32)
    out[...] = raw.astype(bf16)


def keys_kernel(place, sums, taps, weighted_t, logs, keys_out, out):
    raw = sums[...].astype(f32)
    n_taps = taps.shape[0]
    summed = taps[n_taps - 1 :] * raw[HALO:]
    for d in range(1, n_taps):
        summed = summed + taps[n_taps - 1 - d : n_taps - d] * raw[HALO - d : HALO - d + Q]
    keys = (summed / (1.0 + jnp.exp(-summed))).astype(bf16)
    keys_out[...] = keys
    update = jnp.dot(weighted_t[...], keys[:, :N], preferred_element_type=f32).astype(bf16)
    heads = out.shape[0]
    head_width = update.shape[0] // heads
    for h in range(heads):
        out[h, :head_width] = update[h * head_width : (h + 1) * head_width]
        out[h, head_width:] = logs[h]


def total_kernel(place, got, total):
    head_width = got.shape[1] - LOG_ROWS
    rows = got.shape[0] // QUAD
    at = lax.broadcasted_iota(jnp.int32, (LOG_ROWS, N), 0)
    logs = jnp.zeros((LOG_ROWS, N), f32)
    for row in range(rows):
        acc = jnp.zeros((head_width, N), f32)
        log_acc = jnp.zeros((1, N), f32)
        for b in range(QUAD):
            log = log_row(got[row * QUAD + b, head_width:])
            acc = jnp.exp(log) * acc + got[row * QUAD + b, :head_width].astype(f32)
            log_acc = log_acc + log
        total[row * head_width : (row + 1) * head_width] = acc.astype(bf16)
        for i, part in enumerate(split3(log_acc)):
            logs = jnp.where(at == row * 3 + i, part, logs)
    total[rows * head_width :] = logs.astype(bf16)


def states_kernel(place, totals, got, out):
    head_width = out.shape[1]
    rows = out.shape[0] // QUAD
    logs = [totals[quad, rows * head_width :].astype(f32) for quad in range(totals.shape[0])]
    acc = jnp.zeros((head_width, N), f32)
    for row in range(rows):
        carry = acc
        for quad in range(totals.shape[0]):
            carry = jnp.where(place[1] == quad, acc, carry)
            log = jnp.sum(logs[quad][3 * row : 3 * row + 3], axis=0, keepdims=True)
            update = totals[quad, row * head_width : (row + 1) * head_width]
            acc = jnp.exp(log) * acc + update.astype(f32)
        for b in range(QUAD):
            at = row * QUAD + b
            out[at] = carry.astype(bf16)
            if b < QUAD - 1:
                log = log_row(got[at, head_width:])
                carry = jnp.exp(log) * carry + got[at, :head_width].astype(f32)


def within_kernel(place, keys, driven, cum, cum_t, inner, scale, skip, gate, out, grown):
    scores = lax.dot_general(
        keys[:, N:], keys[:, :N], (((1,), (1,)), ((), ())), preferred_element_type=f32
    )
    rows = lax.broadcasted_iota(jnp.int32, (Q, Q), 0)
    cols = lax.broadcasted_iota(jnp.int32, (Q, Q), 1)
    causal = rows >= cols
    heads = cum.shape[1]
    head_width = driven.shape[1] // heads
    per_tile = Q // head_width
    skipped = expand(skip[...], head_width) * scaled_by_tenant(place[3], inner, scale)
    g = gate[...].astype(f32)
    gates = g / (1.0 + jnp.exp(-g))
    grown[...] = gates * expand(jnp.exp(cum[...]), head_width)
    for tile in range(heads // per_tile):
        at = slice(tile * Q, (tile + 1) * Q)
        mixed = None
        for i in range(per_tile):
            h = tile * per_tile + i
            lag = cum[:, h : h + 1] - cum_t[h : h + 1]
            weights = jnp.where(causal, scores * jnp.exp(jnp.where(causal, lag, 0.0)), 0.0)
            summed = jnp.dot(weights.astype(bf16), driven[:, at], preferred_element_type=f32)
            mixed = summed if mixed is None else jnp.where(cols < i * head_width, mixed, summed)
        out[:, at] = (mixed + skipped[:, at]) * gates[:, at]


def output_kernel(place, keys, start, mixed, grown, gain, out):
    width = out.shape[1]
    quarter = width // QUAD
    gated = []
    squares = jnp.zeros((Q, 1), f32)
    for q in range(QUAD):
        at = slice(q * quarter, (q + 1) * quarter)
        carried = lax.dot_general(
            keys[:, N:], start[at], (((1,), (1,)), ((), ())), preferred_element_type=f32
        )
        value = mixed[:, at] + grown[:, at] * carried
        squares = squares + jnp.sum(value * value, axis=1, keepdims=True)
        gated.append(value)
    inverse = lax.rsqrt(squares / width + epsilon)
    for q in range(QUAD):
        at = slice(q * quarter, (q + 1) * quarter)
        out[:, at] = (gated[q] * inverse * gain[:, at].astype(f32)).astype(bf16)


def per_device(
    hidden_states,
    select_weight,
    conv_taps,
    inner_input,
    gate_input,
    step_size,
    decay_rate,
    skip_gain,
    tenant_scale,
    tenant_index,
    norm_gain,
):
    heads = decay_rate.shape[0]
    width = inner_input.shape[1]
    head_width = width // heads
    x, zh, zl = (lax.axis_index(a) for a in CTX)
    place = jnp.stack([x, zh, zl, tenant_index[0]])
    n_z = lax.axis_size(Z)
    n_x = lax.axis_size("x")
    depth = hidden_states.shape[1]

    rows = pl.pallas_call(
        share_kernel,
        out_shape=shape((n_x,) + hidden_states.shape, bf16),
        in_specs=[pl.BlockSpec(memory_space=pl.ANY)],
        out_specs=pl.BlockSpec(memory_space=pl.ANY),
        scratch_shapes=[
            pltpu.VMEM(hidden_states.shape, bf16),
            pltpu.SemaphoreType.DMA,
            pltpu.SemaphoreType.DMA((n_x,)),
        ],
        cost_estimate=pl.CostEstimate(flops=0, bytes_accessed=1_000_000, transcendentals=0),
    )(hidden_states)
    rows = swap(rows, "x")

    n_part = select_weight.shape[1]
    w_zh = lax.all_gather(select_weight.T, "zh", axis=0, tiled=True)
    w_zh, rows = lax.optimization_barrier((w_zh, rows))
    n_core = lax.axis_size("core")
    tails = jnp.pad(
        rows[:, Q - REACH :].reshape(n_x * REACH, depth), ((0, HALO - n_x * REACH), (0, 0))
    )
    w_all = [w_zh] + [
        lax.ppermute(
            jnp.concatenate([w_zh, tails], axis=0) if step == -1 else w_zh,
            Z + ("core",),
            [
                (i * n_core + c, (i - step * (1 if c == 0 else turn)) % n_z * n_core + c)
                for i in range(n_z)
                for c in range(n_core)
            ],
        )
        for step, turn in zip(W_STEPS[1:], (1, 1, -1))
    ]

    driven, cum, cum_t, weighted_t, logs = kernel_call(
        drive_kernel,
        [
            shape((Q, width), bf16),
            shape((Q, heads), f32),
            shape((heads, Q), f32),
            shape((width, Q), bf16),
            shape((heads, LOG_ROWS, N), bf16),
        ],
        place,
        [inner_input, tenant_scale, step_size, decay_rate[None]],
    )


    w_all, weighted_t, logs = lax.optimization_barrier((w_all, weighted_t, logs))

    size = HALO + Q
    sums = kernel_call(
        project_kernel,
        shape((n_x, lax.axis_size("core"), size, 2 * N), bf16),
        place,
        [*w_all, rows],
        [
            pltpu.VMEM((w_zh.shape[0] * QUAD, depth), bf16),
            pltpu.VMEM((n_x * size, depth), bf16),
        ],
    )
    sums = swap(sums.reshape(-1, size, 2 * N), TP)
    sums = to_owner(kernel_call(sum_kernel, shape((size, 2 * N), bf16), place, [sums]))
    keys, update = kernel_call(
        keys_kernel,
        [shape((Q, 2 * N), bf16), shape((heads, head_width + LOG_ROWS, N), bf16)],
        place,
        [sums, conv_taps, weighted_t, logs],
    )

    got = swap(update, NEAR)
    total = kernel_call(
        total_kernel, shape((n_x * head_width + LOG_ROWS, N), bf16), place, [got]
    )
    states = kernel_call(
        states_kernel,
        shape((heads, head_width, N), bf16),
        place,
        [lax.all_gather(total, "zh"), got],
    )
    start = swap(states, NEAR).reshape(width, N)

    mixed, grown = kernel_call(
        within_kernel,
        [shape((Q, width), f32)] * 2,
        place,
        [keys, driven, cum, cum_t, inner_input, tenant_scale, skip_gain[None], gate_input],
    )
    return kernel_call(
        output_kernel,
        shape((Q, width), bf16),
        place,
        [keys, start, mixed, grown, norm_gain[None]],
    )


def solution(mesh):
    fine = Mesh(mesh.devices.reshape(4, 4, 4, 4, 2), CTX + TP)
    in_specs = (
        P(CTX, TP),
        P(TP, CTX),
        P(None, TP),
        P(CTX, TP),
        P(CTX, TP),
        P(CTX, TP),
        P(TP),
        P(TP),
        P(None, TP),
        P(CTX),
        P(TP),
    )
    return jax.shard_map(
        per_device, mesh=fine, in_specs=in_specs, out_specs=P(CTX, TP), check_vma=False
    )
```

```python
import jax
import jax.numpy as jnp
from jax import lax
from jax.experimental import pallas as pl
from jax.experimental.pallas import tpu as pltpu
from jax.sharding import Mesh, PartitionSpec as P

N = 128
Q = 128
QUAD = 4
HALO = 16
REACH = 3
LOG_ROWS = 16
Z = ("zh", "zl")
CTX = ("x",) + Z
NEAR = ("x", "zl")
TP = ("y", "core")

epsilon = 1e-05
bf16 = jnp.bfloat16
f32 = jnp.float32
EXACT = lax.Precision.HIGHEST

VMEM = pl.BlockSpec(memory_space=pltpu.VMEM)
SMEM = pl.BlockSpec(memory_space=pltpu.SMEM)


def swap(blocks, axis):
    return lax.all_to_all(blocks, axis, 0, 0, tiled=True)


def share(block, axis):
    peers = lax.axis_size(axis)
    return swap(jnp.broadcast_to(block[None], (peers,) + block.shape), axis)


def to_owner(block):
    side = lax.axis_size("x")
    pairs = [
        (i * side + j, (j + side // 2) % side * side + i) for i in range(side) for j in range(side)
    ]
    return lax.ppermute(block, ("x", "y"), pairs)


def shape(dims, kind):
    return jax.ShapeDtypeStruct(dims, kind)


def kernel_call(body, outs, place, args, scratch=(), flops=1_000_000):
    return pl.pallas_call(
        body,
        out_shape=outs,
        in_specs=[SMEM] + [VMEM] * len(args),
        out_specs=jax.tree.map(lambda _: VMEM, outs),
        scratch_shapes=scratch,
        compiler_params=pltpu.CompilerParams(vmem_limit_bytes=32 * 1024 * 1024),
        cost_estimate=pl.CostEstimate(flops=flops, bytes_accessed=1_000_000, transcendentals=0),
    )(place, *args)


def expand(columns, head_width):
    heads = columns.shape[1]
    shape2 = (heads, heads * head_width)
    head = lax.broadcasted_iota(jnp.int32, shape2, 0)
    lane = lax.broadcasted_iota(jnp.int32, shape2, 1)
    first = head * head_width
    onehot = jnp.where((lane >= first) & (lane < first + head_width), 1.0, 0.0)
    return jnp.dot(columns, onehot, precision=EXACT, preferred_element_type=f32)


def split3(row):
    hi = row.astype(bf16).astype(f32)
    mid = (row - hi).astype(bf16).astype(f32)
    return hi, mid, row - hi - mid


def log_rows(row):
    hi, mid, low = split3(row)
    at = lax.broadcasted_iota(jnp.int32, (LOG_ROWS, row.shape[1]), 0)
    rows = jnp.where(at == 0, hi, jnp.where(at == 1, mid, jnp.where(at == 2, low, 0.0)))
    return rows.astype(bf16)


def log_row(rows):
    return jnp.sum(rows.astype(f32), axis=0, keepdims=True)


def scaled_by_tenant(tenant, inner_ref, scale_ref):
    row = lax.broadcasted_iota(jnp.int32, scale_ref.shape, 0)
    chosen = jnp.where(row == tenant, scale_ref[...].astype(f32), 0.0)
    return inner_ref[...].astype(f32) * jnp.sum(chosen, axis=0, keepdims=True)


def drive_kernel(place, inner, scale, step, decay, driven, cum, cum_t, weighted_t, logs):
    heads = step.shape[1]
    head_width = inner.shape[1] // heads
    log_decay = -step[...] * decay[...]
    rows = lax.broadcasted_iota(jnp.int32, (Q, Q), 0)
    cols = lax.broadcasted_iota(jnp.int32, (Q, Q), 1)
    lower = jnp.where(rows >= cols, 1.0, 0.0)
    so_far = jnp.dot(lower, log_decay, precision=EXACT, preferred_element_type=f32)
    cum[...] = so_far
    cum_t[...] = lax.dot_general(
        log_decay, lower, (((0,), (1,)), ((), ())), precision=EXACT, preferred_element_type=f32
    )
    end = so_far[Q - 1 :]
    scaled = scaled_by_tenant(place[3], inner, scale)
    drive = (scaled * expand(step[...], head_width)).astype(bf16)
    driven[...] = drive
    tail = expand(jnp.exp(end - so_far), head_width)
    weighted_t[...] = jnp.transpose(tail * drive.astype(f32)).astype(bf16)
    for h in range(heads):
        logs[h] = log_rows(jnp.broadcast_to(end[:, h : h + 1], (1, N)))


def share_kernel(block, out, held, arrived, sent):
    fetch = pltpu.make_async_copy(block, held, arrived)
    fetch.start()
    fetch.wait()
    copies = [pltpu.make_async_copy(held, out.at[i], sent.at[i]) for i in range(out.shape[0])]
    for copy in copies:
        copy.start()
    for copy in copies:
        copy.wait()


def project_kernel(place, own, one, other, across, rows, out, w_in_order, all_rows):
    n_part = N // QUAD
    halves = own.shape[0] // n_part
    zl, core = place[2], place[4]
    steps = (0, 2 * core - 1, 1 - 2 * core, 2)
    for w, step in zip((own, one, other, across), steps):
        s = lax.rem(zl + step + QUAD, QUAD)
        for i in range(halves):
            at = pl.multiple_of(i * N + s * n_part, n_part)
            w_in_order[pl.ds(at, n_part)] = w[i * n_part : (i + 1) * n_part]
    packed = jnp.where(
        core == 0, one[halves * n_part :].astype(f32), other[halves * n_part :].astype(f32)
    )
    tails = [
        pltpu.roll(packed, (HALO - (i + 1) * REACH) % HALO, 0).astype(bf16)
        for i in range(rows.shape[0])
    ]
    first = (place[1] == 0) & (place[2] == 0)
    size = HALO + Q
    for block in range(rows.shape[0]):
        behind = tails[block - 1] if block > 0 else jnp.zeros_like(tails[0])
        all_rows[block * size : block * size + HALO] = jnp.where(first, behind, tails[block])
        all_rows[block * size + HALO : (block + 1) * size] = rows[block]
    for c in range(out.shape[1]):
        sums = lax.dot_general(
            all_rows[...],
            w_in_order[c * 2 * N : (c + 1) * 2 * N],
            (((1,), (1,)), ((), ())),
            preferred_element_type=f32,
        ).astype(bf16)
        for block in range(rows.shape[0]):
            to = (block + rows.shape[0] // 2) % rows.shape[0]
            out[to, c] = sums[block * size : (block + 1) * size]


def sum_kernel(place, parts, out):
    raw = parts[0].astype(f32)
    for i in range(1, parts.shape[0]):
        raw = raw + parts[i].astype(f32)
    out[...] = raw.astype(bf16)


def keys_kernel(place, sums, taps, weighted_t, logs, keys_out, out):
    raw = sums[...].astype(f32)
    n_taps = taps.shape[0]
    summed = taps[n_taps - 1 :] * raw[HALO:]
    for d in range(1, n_taps):
        summed = summed + taps[n_taps - 1 - d : n_taps - d] * raw[HALO - d : HALO - d + Q]
    keys = (summed / (1.0 + jnp.exp(-summed))).astype(bf16)
    keys_out[...] = keys
    update = jnp.dot(weighted_t[...], keys[:, :N], preferred_element_type=f32).astype(bf16)
    heads = out.shape[0]
    head_width = update.shape[0] // heads
    for h in range(heads):
        out[h, :head_width] = update[h * head_width : (h + 1) * head_width]
        out[h, head_width:] = logs[h]


def total_kernel(place, got, total):
    head_width = got.shape[1] - LOG_ROWS
    rows = got.shape[0] // QUAD
    at = lax.broadcasted_iota(jnp.int32, (LOG_ROWS, N), 0)
    logs = jnp.zeros((LOG_ROWS, N), f32)
    for row in range(rows):
        acc = jnp.zeros((head_width, N), f32)
        log_acc = jnp.zeros((1, N), f32)
        for b in range(QUAD):
            log = log_row(got[row * QUAD + b, head_width:])
            acc = jnp.exp(log) * acc + got[row * QUAD + b, :head_width].astype(f32)
            log_acc = log_acc + log
        total[row * head_width : (row + 1) * head_width] = acc.astype(bf16)
        for i, part in enumerate(split3(log_acc)):
            logs = jnp.where(at == row * 3 + i, part, logs)
    total[rows * head_width :] = logs.astype(bf16)


def states_kernel(place, totals, got, out):
    head_width = out.shape[1]
    rows = out.shape[0] // QUAD
    logs = [totals[quad, rows * head_width :].astype(f32) for quad in range(totals.shape[0])]
    acc = jnp.zeros((head_width, N), f32)
    for row in range(rows):
        carry = acc
        for quad in range(totals.shape[0]):
            carry = jnp.where(place[1] == quad, acc, carry)
            log = jnp.sum(logs[quad][3 * row : 3 * row + 3], axis=0, keepdims=True)
            update = totals[quad, row * head_width : (row + 1) * head_width]
            acc = jnp.exp(log) * acc + update.astype(f32)
        for b in range(QUAD):
            at = row * QUAD + b
            out[at] = carry.astype(bf16)
            if b < QUAD - 1:
                log = log_row(got[at, head_width:])
                carry = jnp.exp(log) * carry + got[at, :head_width].astype(f32)


def within_kernel(place, keys, driven, cum, cum_t, inner, scale, skip, gate, out, grown):
    scores = lax.dot_general(
        keys[:, N:], keys[:, :N], (((1,), (1,)), ((), ())), preferred_element_type=f32
    )
    rows = lax.broadcasted_iota(jnp.int32, (Q, Q), 0)
    cols = lax.broadcasted_iota(jnp.int32, (Q, Q), 1)
    causal = rows >= cols
    heads = cum.shape[1]
    head_width = driven.shape[1] // heads
    per_tile = Q // head_width
    skipped = expand(skip[...], head_width) * scaled_by_tenant(place[3], inner, scale)
    g = gate[...].astype(f32)
    gates = g / (1.0 + jnp.exp(-g))
    grown[...] = gates * expand(jnp.exp(cum[...]), head_width)
    for tile in range(heads // per_tile):
        at = slice(tile * Q, (tile + 1) * Q)
        mixed = None
        for i in range(per_tile):
            h = tile * per_tile + i
            lag = cum[:, h : h + 1] - cum_t[h : h + 1]
            weights = jnp.where(causal, scores * jnp.exp(jnp.where(causal, lag, 0.0)), 0.0)
            summed = jnp.dot(weights.astype(bf16), driven[:, at], preferred_element_type=f32)
            mixed = summed if mixed is None else jnp.where(cols < i * head_width, mixed, summed)
        out[:, at] = (mixed + skipped[:, at]) * gates[:, at]


def output_kernel(place, keys, start, mixed, grown, gain, out):
    width = out.shape[1]
    quarter = width // QUAD
    gated = []
    squares = jnp.zeros((Q, 1), f32)
    for q in range(QUAD):
        at = slice(q * quarter, (q + 1) * quarter)
        carried = lax.dot_general(
            keys[:, N:], start[at], (((1,), (1,)), ((), ())), preferred_element_type=f32
        )
        value = mixed[:, at] + grown[:, at] * carried
        squares = squares + jnp.sum(value * value, axis=1, keepdims=True)
        gated.append(value)
    inverse = lax.rsqrt(squares / width + epsilon)
    for q in range(QUAD):
        at = slice(q * quarter, (q + 1) * quarter)
        out[:, at] = (gated[q] * inverse * gain[:, at].astype(f32)).astype(bf16)


def per_device(
    hidden_states,
    select_weight,
    conv_taps,
    inner_input,
    gate_input,
    step_size,
    decay_rate,
    skip_gain,
    tenant_scale,
    tenant_index,
    norm_gain,
):
    heads = decay_rate.shape[0]
    width = inner_input.shape[1]
    head_width = width // heads
    x, zh, zl = (lax.axis_index(a) for a in CTX)
    place = jnp.stack([x, zh, zl, tenant_index[0], lax.axis_index("core")])
    n_z = lax.axis_size(Z)
    n_x = lax.axis_size("x")
    depth = hidden_states.shape[1]

    rows = pl.pallas_call(
        share_kernel,
        out_shape=shape((n_x,) + hidden_states.shape, bf16),
        in_specs=[pl.BlockSpec(memory_space=pl.ANY)],
        out_specs=pl.BlockSpec(memory_space=pl.ANY),
        scratch_shapes=[
            pltpu.VMEM(hidden_states.shape, bf16),
            pltpu.SemaphoreType.DMA,
            pltpu.SemaphoreType.DMA((n_x,)),
        ],
        cost_estimate=pl.CostEstimate(flops=0, bytes_accessed=1_000_000, transcendentals=0),
    )(hidden_states)
    rows = swap(rows, "x")

    n_part = select_weight.shape[1]
    w_zh = lax.all_gather(select_weight.T, "zh", axis=0, tiled=True)
    w_zh, rows = lax.optimization_barrier((w_zh, rows))
    n_core = lax.axis_size("core")
    tails = jnp.pad(
        rows[:, Q - REACH :].reshape(n_x * REACH, depth), ((0, HALO - n_x * REACH), (0, 0))
    )
    both = jnp.concatenate([w_zh, tails], axis=0)

    def from_side(block, step):
        pairs = [
            (i * n_core + c, (i + step * (1 - 2 * c)) % n_z * n_core + c)
            for i in range(n_z)
            for c in range(n_core)
        ]
        return lax.ppermute(block, Z + ("core",), pairs)

    w_all = [w_zh, from_side(both, 1), from_side(both, -1), from_side(w_zh, 2)]

    driven, cum, cum_t, weighted_t, logs = kernel_call(
        drive_kernel,
        [
            shape((Q, width), bf16),
            shape((Q, heads), f32),
            shape((heads, Q), f32),
            shape((width, Q), bf16),
            shape((heads, LOG_ROWS, N), bf16),
        ],
        place,
        [inner_input, tenant_scale, step_size, decay_rate[None]],
    )


    w_all, weighted_t, logs = lax.optimization_barrier((w_all, weighted_t, logs))

    size = HALO + Q
    sums = kernel_call(
        project_kernel,
        shape((n_x, lax.axis_size("core"), size, 2 * N), bf16),
        place,
        [*w_all, rows],
        [
            pltpu.VMEM((w_zh.shape[0] * QUAD, depth), bf16),
            pltpu.VMEM((n_x * size, depth), bf16),
        ],
    )
    sums = swap(sums.reshape(-1, size, 2 * N), TP)
    sums = to_owner(kernel_call(sum_kernel, shape((size, 2 * N), bf16), place, [sums]))
    keys, update = kernel_call(
        keys_kernel,
        [shape((Q, 2 * N), bf16), shape((heads, head_width + LOG_ROWS, N), bf16)],
        place,
        [sums, conv_taps, weighted_t, logs],
    )

    got = swap(update, NEAR)
    total = kernel_call(
        total_kernel, shape((n_x * head_width + LOG_ROWS, N), bf16), place, [got]
    )
    states = kernel_call(
        states_kernel,
        shape((heads, head_width, N), bf16),
        place,
        [lax.all_gather(total, "zh"), got],
    )
    start = swap(states, NEAR).reshape(width, N)

    mixed, grown = kernel_call(
        within_kernel,
        [shape((Q, width), f32)] * 2,
        place,
        [keys, driven, cum, cum_t, inner_input, tenant_scale, skip_gain[None], gate_input],
    )
    return kernel_call(
        output_kernel,
        shape((Q, width), bf16),
        place,
        [keys, start, mixed, grown, norm_gain[None]],
    )


def solution(mesh):
    fine = Mesh(mesh.devices.reshape(4, 4, 4, 4, 2), CTX + TP)
    in_specs = (
        P(CTX, TP),
        P(TP, CTX),
        P(None, TP),
        P(CTX, TP),
        P(CTX, TP),
        P(CTX, TP),
        P(TP),
        P(TP),
        P(None, TP),
        P(CTX),
        P(TP),
    )
    return jax.shard_map(
        per_device, mesh=fine, in_specs=in_specs, out_specs=P(CTX, TP), check_vma=False
    )
```

```python
import jax
import jax.numpy as jnp
from jax import lax
from jax.experimental import pallas as pl
from jax.experimental.pallas import tpu as pltpu
from jax.sharding import Mesh, PartitionSpec as P

N = 128
Q = 128
QUAD = 4
HALO = 16
REACH = 3
LOG_ROWS = 16
Z = ("zh", "zl")
CTX = ("x",) + Z
NEAR = ("x", "zl")
TP = ("y", "core")

epsilon = 1e-05
bf16 = jnp.bfloat16
f32 = jnp.float32
EXACT = lax.Precision.HIGHEST

VMEM = pl.BlockSpec(memory_space=pltpu.VMEM)
SMEM = pl.BlockSpec(memory_space=pltpu.SMEM)


def swap(blocks, axis):
    return lax.all_to_all(blocks, axis, 0, 0, tiled=True)


def share(block, axis):
    peers = lax.axis_size(axis)
    return swap(jnp.broadcast_to(block[None], (peers,) + block.shape), axis)


def to_owner(block):
    side = lax.axis_size("x")
    pairs = [
        (i * side + j, (j + side // 2) % side * side + i) for i in range(side) for j in range(side)
    ]
    return lax.ppermute(block, ("x", "y"), pairs)


def shape(dims, kind):
    return jax.ShapeDtypeStruct(dims, kind)


def kernel_call(body, outs, place, args, scratch=(), flops=1_000_000):
    return pl.pallas_call(
        body,
        out_shape=outs,
        in_specs=[SMEM] + [VMEM] * len(args),
        out_specs=jax.tree.map(lambda _: VMEM, outs),
        scratch_shapes=scratch,
        compiler_params=pltpu.CompilerParams(vmem_limit_bytes=32 * 1024 * 1024),
        cost_estimate=pl.CostEstimate(flops=flops, bytes_accessed=1_000_000, transcendentals=0),
    )(place, *args)


def expand(columns, head_width):
    heads = columns.shape[1]
    shape2 = (heads, heads * head_width)
    head = lax.broadcasted_iota(jnp.int32, shape2, 0)
    lane = lax.broadcasted_iota(jnp.int32, shape2, 1)
    first = head * head_width
    onehot = jnp.where((lane >= first) & (lane < first + head_width), 1.0, 0.0)
    return jnp.dot(columns, onehot, precision=EXACT, preferred_element_type=f32)


def split3(row):
    hi = row.astype(bf16).astype(f32)
    mid = (row - hi).astype(bf16).astype(f32)
    return hi, mid, row - hi - mid


def log_rows(row):
    hi, mid, low = split3(row)
    at = lax.broadcasted_iota(jnp.int32, (LOG_ROWS, row.shape[1]), 0)
    rows = jnp.where(at == 0, hi, jnp.where(at == 1, mid, jnp.where(at == 2, low, 0.0)))
    return rows.astype(bf16)


def log_row(rows):
    return jnp.sum(rows.astype(f32), axis=0, keepdims=True)


def scaled_by_tenant(tenant, inner_ref, scale_ref):
    row = lax.broadcasted_iota(jnp.int32, scale_ref.shape, 0)
    chosen = jnp.where(row == tenant, scale_ref[...].astype(f32), 0.0)
    return inner_ref[...].astype(f32) * jnp.sum(chosen, axis=0, keepdims=True)


def drive_kernel(place, inner, scale, step, decay, driven, cum, cum_t, weighted_t, logs):
    heads = step.shape[1]
    head_width = inner.shape[1] // heads
    log_decay = -step[...] * decay[...]
    rows = lax.broadcasted_iota(jnp.int32, (Q, Q), 0)
    cols = lax.broadcasted_iota(jnp.int32, (Q, Q), 1)
    lower = jnp.where(rows >= cols, 1.0, 0.0)
    so_far = jnp.dot(lower, log_decay, precision=EXACT, preferred_element_type=f32)
    cum[...] = so_far
    cum_t[...] = lax.dot_general(
        so_far,
        jnp.where(rows == cols, 1.0, 0.0),
        (((0,), (0,)), ((), ())),
        precision=EXACT,
        preferred_element_type=f32,
    )
    end = so_far[Q - 1 :]
    scaled = scaled_by_tenant(place[3], inner, scale)
    drive = (scaled * expand(step[...], head_width)).astype(bf16)
    driven[...] = drive
    tail = expand(jnp.exp(end - so_far), head_width)
    weighted_t[...] = jnp.transpose(tail * drive.astype(f32)).astype(bf16)
    for h in range(heads):
        logs[h] = log_rows(jnp.broadcast_to(end[:, h : h + 1], (1, N)))


def share_kernel(block, out, held, arrived, sent):
    fetch = pltpu.make_async_copy(block, held, arrived)
    fetch.start()
    fetch.wait()
    copies = [pltpu.make_async_copy(held, out.at[i], sent.at[i]) for i in range(out.shape[0])]
    for copy in copies:
        copy.start()
    for copy in copies:
        copy.wait()


def project_kernel(place, own, one, other, across, rows, out, w_in_order, all_rows):
    n_part = N // QUAD
    halves = own.shape[0] // n_part
    zl, core = place[2], place[4]
    steps = (0, 2 * core - 1, 1 - 2 * core, 2)
    for w, step in zip((own, one, other, across), steps):
        s = lax.rem(zl + step + QUAD, QUAD)
        for i in range(halves):
            at = pl.multiple_of(i * N + s * n_part, n_part)
            w_in_order[pl.ds(at, n_part)] = w[i * n_part : (i + 1) * n_part]
    packed = jnp.where(
        core == 0, one[halves * n_part :].astype(f32), other[halves * n_part :].astype(f32)
    )
    tails = [
        pltpu.roll(packed, (HALO - (i + 1) * REACH) % HALO, 0).astype(bf16)
        for i in range(rows.shape[0])
    ]
    first = (place[1] == 0) & (place[2] == 0)
    size = HALO + Q
    for block in range(rows.shape[0]):
        behind = tails[block - 1] if block > 0 else jnp.zeros_like(tails[0])
        all_rows[block * size : block * size + HALO] = jnp.where(first, behind, tails[block])
        all_rows[block * size + HALO : (block + 1) * size] = rows[block]
    for c in range(out.shape[1]):
        sums = lax.dot_general(
            all_rows[...],
            w_in_order[c * 2 * N : (c + 1) * 2 * N],
            (((1,), (1,)), ((), ())),
            preferred_element_type=f32,
        ).astype(bf16)
        for block in range(rows.shape[0]):
            to = (block + rows.shape[0] // 2) % rows.shape[0]
            out[to, c] = sums[block * size : (block + 1) * size]


def sum_kernel(place, parts, out):
    raw = parts[0].astype(f32)
    for i in range(1, parts.shape[0]):
        raw = raw + parts[i].astype(f32)
    out[...] = raw.astype(bf16)


def keys_kernel(place, sums, taps, weighted_t, logs, keys_out, out):
    raw = sums[...].astype(f32)
    n_taps = taps.shape[0]
    summed = taps[n_taps - 1 :] * raw[HALO:]
    for d in range(1, n_taps):
        summed = summed + taps[n_taps - 1 - d : n_taps - d] * raw[HALO - d : HALO - d + Q]
    keys = (summed / (1.0 + jnp.exp(-summed))).astype(bf16)
    keys_out[...] = keys
    update = jnp.dot(weighted_t[...], keys[:, :N], preferred_element_type=f32).astype(bf16)
    heads = out.shape[0]
    head_width = update.shape[0] // heads
    for h in range(heads):
        out[h, :head_width] = update[h * head_width : (h + 1) * head_width]
        out[h, head_width:] = logs[h]


def total_kernel(place, got, total):
    head_width = got.shape[1] - LOG_ROWS
    rows = got.shape[0] // QUAD
    at = lax.broadcasted_iota(jnp.int32, (LOG_ROWS, N), 0)
    logs = jnp.zeros((LOG_ROWS, N), f32)
    for row in range(rows):
        acc = jnp.zeros((head_width, N), f32)
        log_acc = jnp.zeros((1, N), f32)
        for b in range(QUAD):
            log = log_row(got[row * QUAD + b, head_width:])
            acc = jnp.exp(log) * acc + got[row * QUAD + b, :head_width].astype(f32)
            log_acc = log_acc + log
        total[row * head_width : (row + 1) * head_width] = acc.astype(bf16)
        for i, part in enumerate(split3(log_acc)):
            logs = jnp.where(at == row * 3 + i, part, logs)
    total[rows * head_width :] = logs.astype(bf16)


def states_kernel(place, totals, got, out):
    head_width = out.shape[1]
    rows = out.shape[0] // QUAD
    logs = [totals[quad, rows * head_width :].astype(f32) for quad in range(totals.shape[0])]
    acc = jnp.zeros((head_width, N), f32)
    for row in range(rows):
        carry = acc
        for quad in range(totals.shape[0]):
            carry = jnp.where(place[1] == quad, acc, carry)
            log = jnp.sum(logs[quad][3 * row : 3 * row + 3], axis=0, keepdims=True)
            update = totals[quad, row * head_width : (row + 1) * head_width]
            acc = jnp.exp(log) * acc + update.astype(f32)
        for b in range(QUAD):
            at = row * QUAD + b
            out[at] = carry.astype(bf16)
            if b < QUAD - 1:
                log = log_row(got[at, head_width:])
                carry = jnp.exp(log) * carry + got[at, :head_width].astype(f32)


def within_kernel(place, keys, driven, cum, cum_t, inner, scale, skip, gate, out, grown):
    scores = lax.dot_general(
        keys[:, N:], keys[:, :N], (((1,), (1,)), ((), ())), preferred_element_type=f32
    )
    rows = lax.broadcasted_iota(jnp.int32, (Q, Q), 0)
    cols = lax.broadcasted_iota(jnp.int32, (Q, Q), 1)
    causal = rows >= cols
    heads = cum.shape[1]
    head_width = driven.shape[1] // heads
    per_tile = Q // head_width
    skipped = expand(skip[...], head_width) * scaled_by_tenant(place[3], inner, scale)
    g = gate[...].astype(f32)
    gates = g / (1.0 + jnp.exp(-g))
    grown[...] = gates * expand(jnp.exp(cum[...]), head_width)
    for tile in range(heads // per_tile):
        at = slice(tile * Q, (tile + 1) * Q)
        mixed = None
        for i in range(per_tile):
            h = tile * per_tile + i
            lag = cum[:, h : h + 1] - cum_t[h : h + 1]
            weights = jnp.where(causal, scores * jnp.exp(jnp.where(causal, lag, 0.0)), 0.0)
            summed = jnp.dot(weights.astype(bf16), driven[:, at], preferred_element_type=f32)
            mixed = summed if mixed is None else jnp.where(cols < i * head_width, mixed, summed)
        out[:, at] = (mixed + skipped[:, at]) * gates[:, at]


def output_kernel(place, keys, start, mixed, grown, gain, out):
    width = out.shape[1]
    quarter = width // QUAD
    gated = []
    squares = jnp.zeros((Q, 1), f32)
    for q in range(QUAD):
        at = slice(q * quarter, (q + 1) * quarter)
        carried = lax.dot_general(
            keys[:, N:], start[at], (((1,), (1,)), ((), ())), preferred_element_type=f32
        )
        value = mixed[:, at] + grown[:, at] * carried
        squares = squares + jnp.sum(value * value, axis=1, keepdims=True)
        gated.append(value)
    inverse = lax.rsqrt(squares / width + epsilon)
    for q in range(QUAD):
        at = slice(q * quarter, (q + 1) * quarter)
        out[:, at] = (gated[q] * inverse * gain[:, at].astype(f32)).astype(bf16)


def per_device(
    hidden_states,
    select_weight,
    conv_taps,
    inner_input,
    gate_input,
    step_size,
    decay_rate,
    skip_gain,
    tenant_scale,
    tenant_index,
    norm_gain,
):
    heads = decay_rate.shape[0]
    width = inner_input.shape[1]
    head_width = width // heads
    x, zh, zl = (lax.axis_index(a) for a in CTX)
    place = jnp.stack([x, zh, zl, tenant_index[0], lax.axis_index("core")])
    n_z = lax.axis_size(Z)
    n_x = lax.axis_size("x")
    depth = hidden_states.shape[1]

    rows = pl.pallas_call(
        share_kernel,
        out_shape=shape((n_x,) + hidden_states.shape, bf16),
        in_specs=[pl.BlockSpec(memory_space=pl.ANY)],
        out_specs=pl.BlockSpec(memory_space=pl.ANY),
        scratch_shapes=[
            pltpu.VMEM(hidden_states.shape, bf16),
            pltpu.SemaphoreType.DMA,
            pltpu.SemaphoreType.DMA((n_x,)),
        ],
        cost_estimate=pl.CostEstimate(flops=0, bytes_accessed=1_000_000, transcendentals=0),
    )(hidden_states)
    rows = swap(rows, "x")

    n_part = select_weight.shape[1]
    w_zh = lax.all_gather(select_weight.T, "zh", axis=0, tiled=True)
    w_zh, rows = lax.optimization_barrier((w_zh, rows))
    n_core = lax.axis_size("core")
    tails = jnp.pad(
        rows[:, Q - REACH :].reshape(n_x * REACH, depth), ((0, HALO - n_x * REACH), (0, 0))
    )
    both = jnp.concatenate([w_zh, tails], axis=0)

    def from_side(block, step):
        pairs = [
            (i * n_core + c, (i + step * (1 - 2 * c)) % n_z * n_core + c)
            for i in range(n_z)
            for c in range(n_core)
        ]
        return lax.ppermute(block, Z + ("core",), pairs)

    w_all = [w_zh, from_side(both, 1), from_side(both, -1), from_side(w_zh, 2)]

    driven, cum, cum_t, weighted_t, logs = kernel_call(
        drive_kernel,
        [
            shape((Q, width), bf16),
            shape((Q, heads), f32),
            shape((heads, Q), f32),
            shape((width, Q), bf16),
            shape((heads, LOG_ROWS, N), bf16),
        ],
        place,
        [inner_input, tenant_scale, step_size, decay_rate[None]],
    )


    w_all, weighted_t, logs = lax.optimization_barrier((w_all, weighted_t, logs))

    size = HALO + Q
    sums = kernel_call(
        project_kernel,
        shape((n_x, lax.axis_size("core"), size, 2 * N), bf16),
        place,
        [*w_all, rows],
        [
            pltpu.VMEM((w_zh.shape[0] * QUAD, depth), bf16),
            pltpu.VMEM((n_x * size, depth), bf16),
        ],
    )
    sums = swap(sums.reshape(-1, size, 2 * N), TP)
    sums = to_owner(kernel_call(sum_kernel, shape((size, 2 * N), bf16), place, [sums]))
    keys, update = kernel_call(
        keys_kernel,
        [shape((Q, 2 * N), bf16), shape((heads, head_width + LOG_ROWS, N), bf16)],
        place,
        [sums, conv_taps, weighted_t, logs],
    )

    got = swap(update, NEAR)
    total = kernel_call(
        total_kernel, shape((n_x * head_width + LOG_ROWS, N), bf16), place, [got]
    )
    states = kernel_call(
        states_kernel,
        shape((heads, head_width, N), bf16),
        place,
        [lax.all_gather(total, "zh"), got],
    )
    start = swap(states, NEAR).reshape(width, N)

    mixed, grown = kernel_call(
        within_kernel,
        [shape((Q, width), f32)] * 2,
        place,
        [keys, driven, cum, cum_t, inner_input, tenant_scale, skip_gain[None], gate_input],
    )
    return kernel_call(
        output_kernel,
        shape((Q, width), bf16),
        place,
        [keys, start, mixed, grown, norm_gain[None]],
    )


def solution(mesh):
    fine = Mesh(mesh.devices.reshape(4, 4, 4, 4, 2), CTX + TP)
    in_specs = (
        P(CTX, TP),
        P(TP, CTX),
        P(None, TP),
        P(CTX, TP),
        P(CTX, TP),
        P(CTX, TP),
        P(TP),
        P(TP),
        P(None, TP),
        P(CTX),
        P(TP),
    )
    return jax.shard_map(
        per_device, mesh=fine, in_specs=in_specs, out_specs=P(CTX, TP), check_vma=False
    )
```

```python
import jax
import jax.numpy as jnp
from jax import lax
from jax.experimental import pallas as pl
from jax.experimental.pallas import tpu as pltpu
from jax.sharding import Mesh, PartitionSpec as P

N = 128
Q = 128
QUAD = 4
HALO = 16
REACH = 3
LOG_ROWS = 16
Z = ("zh", "zl")
CTX = ("x",) + Z
NEAR = ("x", "zl")
TP = ("y", "core")

epsilon = 1e-05
bf16 = jnp.bfloat16
f32 = jnp.float32
EXACT = lax.Precision.HIGHEST

VMEM = pl.BlockSpec(memory_space=pltpu.VMEM)
SMEM = pl.BlockSpec(memory_space=pltpu.SMEM)


def swap(blocks, axis):
    return lax.all_to_all(blocks, axis, 0, 0, tiled=True)


def share(block, axis):
    peers = lax.axis_size(axis)
    return swap(jnp.broadcast_to(block[None], (peers,) + block.shape), axis)


def to_owner(block):
    side = lax.axis_size("x")
    pairs = [
        (i * side + j, (j + side // 2) % side * side + i) for i in range(side) for j in range(side)
    ]
    return lax.ppermute(block, ("x", "y"), pairs)


def shape(dims, kind):
    return jax.ShapeDtypeStruct(dims, kind)


def kernel_call(body, outs, scalars, args, scratch=(), flops=1_000_000):
    placed = [] if scalars is None else [scalars]
    return pl.pallas_call(
        body,
        out_shape=outs,
        in_specs=[SMEM] * len(placed) + [VMEM] * len(args),
        out_specs=jax.tree.map(lambda _: VMEM, outs),
        scratch_shapes=scratch,
        compiler_params=pltpu.CompilerParams(vmem_limit_bytes=32 * 1024 * 1024),
        cost_estimate=pl.CostEstimate(flops=flops, bytes_accessed=1_000_000, transcendentals=0),
    )(*placed, *args)


def expand(columns, head_width):
    heads = columns.shape[1]
    shape2 = (heads, heads * head_width)
    head = lax.broadcasted_iota(jnp.int32, shape2, 0)
    lane = lax.broadcasted_iota(jnp.int32, shape2, 1)
    first = head * head_width
    onehot = jnp.where((lane >= first) & (lane < first + head_width), 1.0, 0.0)
    return jnp.dot(columns, onehot, precision=EXACT, preferred_element_type=f32)


def split3(row):
    hi = row.astype(bf16).astype(f32)
    mid = (row - hi).astype(bf16).astype(f32)
    return hi, mid, row - hi - mid


def log_rows(row):
    hi, mid, low = split3(row)
    at = lax.broadcasted_iota(jnp.int32, (LOG_ROWS, row.shape[1]), 0)
    rows = jnp.where(at == 0, hi, jnp.where(at == 1, mid, jnp.where(at == 2, low, 0.0)))
    return rows.astype(bf16)


def log_row(rows):
    return jnp.sum(rows.astype(f32), axis=0, keepdims=True)


def scaled_by_tenant(tenant, inner_ref, scale_ref):
    row = lax.broadcasted_iota(jnp.int32, scale_ref.shape, 0)
    chosen = jnp.where(row == tenant, scale_ref[...].astype(f32), 0.0)
    return inner_ref[...].astype(f32) * jnp.sum(chosen, axis=0, keepdims=True)


def drive_kernel(tenant, inner, scale, step, decay, driven, cum, cum_t, weighted_t, logs):
    heads = step.shape[1]
    head_width = inner.shape[1] // heads
    log_decay = -step[...] * decay[...]
    rows = lax.broadcasted_iota(jnp.int32, (Q, Q), 0)
    cols = lax.broadcasted_iota(jnp.int32, (Q, Q), 1)
    lower = jnp.where(rows >= cols, 1.0, 0.0)
    so_far = jnp.dot(lower, log_decay, precision=EXACT, preferred_element_type=f32)
    cum[...] = so_far
    cum_t[...] = lax.dot_general(
        so_far,
        jnp.where(rows == cols, 1.0, 0.0),
        (((0,), (0,)), ((), ())),
        precision=EXACT,
        preferred_element_type=f32,
    )
    end = so_far[Q - 1 :]
    scaled = scaled_by_tenant(tenant[0], inner, scale)
    drive = (scaled * expand(step[...], head_width)).astype(bf16)
    driven[...] = drive
    tail = expand(jnp.exp(end - so_far), head_width)
    weighted_t[...] = jnp.transpose(tail * drive.astype(f32)).astype(bf16)
    for h in range(heads):
        logs[h] = log_rows(jnp.broadcast_to(end[:, h : h + 1], (1, N)))


def share_kernel(block, out, held, arrived, sent):
    fetch = pltpu.make_async_copy(block, held, arrived)
    fetch.start()
    fetch.wait()
    copies = [pltpu.make_async_copy(held, out.at[i], sent.at[i]) for i in range(out.shape[0])]
    for copy in copies:
        copy.start()
    for copy in copies:
        copy.wait()


def project_kernel(own, one, other, across, rows, out, w_in_order, all_rows):
    n_part = N // QUAD
    halves = own.shape[0] // n_part
    zh, zl, core = (lax.axis_index(a) for a in Z + ("core",))
    steps = (0, 2 * core - 1, 1 - 2 * core, 2)
    for w, step in zip((own, one, other, across), steps):
        s = lax.rem(zl + step + QUAD, QUAD)
        for i in range(halves):
            at = pl.multiple_of(i * N + s * n_part, n_part)
            w_in_order[pl.ds(at, n_part)] = w[i * n_part : (i + 1) * n_part]
    packed = jnp.where(
        core == 0, one[halves * n_part :].astype(f32), other[halves * n_part :].astype(f32)
    )
    tails = [
        pltpu.roll(packed, (HALO - (i + 1) * REACH) % HALO, 0).astype(bf16)
        for i in range(rows.shape[0])
    ]
    first = (zh == 0) & (zl == 0)
    size = HALO + Q
    for block in range(rows.shape[0]):
        behind = tails[block - 1] if block > 0 else jnp.zeros_like(tails[0])
        all_rows[block * size : block * size + HALO] = jnp.where(first, behind, tails[block])
        all_rows[block * size + HALO : (block + 1) * size] = rows[block]
    for c in range(out.shape[1]):
        sums = lax.dot_general(
            all_rows[...],
            w_in_order[c * 2 * N : (c + 1) * 2 * N],
            (((1,), (1,)), ((), ())),
            preferred_element_type=f32,
        ).astype(bf16)
        for block in range(rows.shape[0]):
            to = (block + rows.shape[0] // 2) % rows.shape[0]
            out[to, c] = sums[block * size : (block + 1) * size]


def sum_kernel(parts, out):
    raw = parts[0].astype(f32)
    for i in range(1, parts.shape[0]):
        raw = raw + parts[i].astype(f32)
    out[...] = raw.astype(bf16)


def keys_kernel(sums, taps, weighted_t, logs, keys_out, out):
    raw = sums[...].astype(f32)
    n_taps = taps.shape[0]
    summed = taps[n_taps - 1 :] * raw[HALO:]
    for d in range(1, n_taps):
        summed = summed + taps[n_taps - 1 - d : n_taps - d] * raw[HALO - d : HALO - d + Q]
    keys = (summed / (1.0 + jnp.exp(-summed))).astype(bf16)
    keys_out[...] = keys
    update = jnp.dot(weighted_t[...], keys[:, :N], preferred_element_type=f32).astype(bf16)
    heads = out.shape[0]
    head_width = update.shape[0] // heads
    for h in range(heads):
        out[h, :head_width] = update[h * head_width : (h + 1) * head_width]
        out[h, head_width:] = logs[h]


def total_kernel(got, total):
    head_width = got.shape[1] - LOG_ROWS
    rows = got.shape[0] // QUAD
    at = lax.broadcasted_iota(jnp.int32, (LOG_ROWS, N), 0)
    logs = jnp.zeros((LOG_ROWS, N), f32)
    for row in range(rows):
        acc = jnp.zeros((head_width, N), f32)
        log_acc = jnp.zeros((1, N), f32)
        for b in range(QUAD):
            log = log_row(got[row * QUAD + b, head_width:])
            acc = jnp.exp(log) * acc + got[row * QUAD + b, :head_width].astype(f32)
            log_acc = log_acc + log
        total[row * head_width : (row + 1) * head_width] = acc.astype(bf16)
        for i, part in enumerate(split3(log_acc)):
            logs = jnp.where(at == row * 3 + i, part, logs)
    total[rows * head_width :] = logs.astype(bf16)


def states_kernel(totals, got, out):
    zh = lax.axis_index("zh")
    head_width = out.shape[1]
    rows = out.shape[0] // QUAD
    logs = [totals[quad, rows * head_width :].astype(f32) for quad in range(totals.shape[0])]
    acc = jnp.zeros((head_width, N), f32)
    for row in range(rows):
        carry = acc
        for quad in range(totals.shape[0]):
            carry = jnp.where(zh == quad, acc, carry)
            log = jnp.sum(logs[quad][3 * row : 3 * row + 3], axis=0, keepdims=True)
            update = totals[quad, row * head_width : (row + 1) * head_width]
            acc = jnp.exp(log) * acc + update.astype(f32)
        for b in range(QUAD):
            at = row * QUAD + b
            out[at] = carry.astype(bf16)
            if b < QUAD - 1:
                log = log_row(got[at, head_width:])
                carry = jnp.exp(log) * carry + got[at, :head_width].astype(f32)


def within_kernel(tenant, keys, driven, cum, cum_t, inner, scale, skip, gate, out, grown):
    scores = lax.dot_general(
        keys[:, N:], keys[:, :N], (((1,), (1,)), ((), ())), preferred_element_type=f32
    )
    rows = lax.broadcasted_iota(jnp.int32, (Q, Q), 0)
    cols = lax.broadcasted_iota(jnp.int32, (Q, Q), 1)
    causal = rows >= cols
    heads = cum.shape[1]
    head_width = driven.shape[1] // heads
    per_tile = Q // head_width
    skipped = expand(skip[...], head_width) * scaled_by_tenant(tenant[0], inner, scale)
    g = gate[...].astype(f32)
    gates = g / (1.0 + jnp.exp(-g))
    grown[...] = gates * expand(jnp.exp(cum[...]), head_width)
    for tile in range(heads // per_tile):
        at = slice(tile * Q, (tile + 1) * Q)
        mixed = None
        for i in range(per_tile):
            h = tile * per_tile + i
            lag = cum[:, h : h + 1] - cum_t[h : h + 1]
            weights = jnp.where(causal, scores * jnp.exp(jnp.where(causal, lag, 0.0)), 0.0)
            summed = jnp.dot(weights.astype(bf16), driven[:, at], preferred_element_type=f32)
            mixed = summed if mixed is None else jnp.where(cols < i * head_width, mixed, summed)
        out[:, at] = (mixed + skipped[:, at]) * gates[:, at]


def output_kernel(keys, start, mixed, grown, gain, out):
    width = out.shape[1]
    quarter = width // QUAD
    gated = []
    squares = jnp.zeros((Q, 1), f32)
    for q in range(QUAD):
        at = slice(q * quarter, (q + 1) * quarter)
        carried = lax.dot_general(
            keys[:, N:], start[at], (((1,), (1,)), ((), ())), preferred_element_type=f32
        )
        value = mixed[:, at] + grown[:, at] * carried
        squares = squares + jnp.sum(value * value, axis=1, keepdims=True)
        gated.append(value)
    inverse = lax.rsqrt(squares / width + epsilon)
    for q in range(QUAD):
        at = slice(q * quarter, (q + 1) * quarter)
        out[:, at] = (gated[q] * inverse * gain[:, at].astype(f32)).astype(bf16)


def per_device(
    hidden_states,
    select_weight,
    conv_taps,
    inner_input,
    gate_input,
    step_size,
    decay_rate,
    skip_gain,
    tenant_scale,
    tenant_index,
    norm_gain,
):
    heads = decay_rate.shape[0]
    width = inner_input.shape[1]
    head_width = width // heads
    n_z = lax.axis_size(Z)
    n_x = lax.axis_size("x")
    depth = hidden_states.shape[1]

    rows = pl.pallas_call(
        share_kernel,
        out_shape=shape((n_x,) + hidden_states.shape, bf16),
        in_specs=[pl.BlockSpec(memory_space=pl.ANY)],
        out_specs=pl.BlockSpec(memory_space=pl.ANY),
        scratch_shapes=[
            pltpu.VMEM(hidden_states.shape, bf16),
            pltpu.SemaphoreType.DMA,
            pltpu.SemaphoreType.DMA((n_x,)),
        ],
        cost_estimate=pl.CostEstimate(flops=0, bytes_accessed=1_000_000, transcendentals=0),
    )(hidden_states)
    rows = swap(rows, "x")

    n_part = select_weight.shape[1]
    w_zh = lax.all_gather(select_weight.T, "zh", axis=0, tiled=True)
    w_zh, rows = lax.optimization_barrier((w_zh, rows))
    n_core = lax.axis_size("core")
    tails = jnp.pad(
        rows[:, Q - REACH :].reshape(n_x * REACH, depth), ((0, HALO - n_x * REACH), (0, 0))
    )
    both = jnp.concatenate([w_zh, tails], axis=0)

    def from_side(block, step):
        pairs = [
            (i * n_core + c, (i + step * (1 - 2 * c)) % n_z * n_core + c)
            for i in range(n_z)
            for c in range(n_core)
        ]
        return lax.ppermute(block, Z + ("core",), pairs)

    w_all = [w_zh, from_side(both, 1), from_side(both, -1), from_side(w_zh, 2)]

    driven, cum, cum_t, weighted_t, logs = kernel_call(
        drive_kernel,
        [
            shape((Q, width), bf16),
            shape((Q, heads), f32),
            shape((heads, Q), f32),
            shape((width, Q), bf16),
            shape((heads, LOG_ROWS, N), bf16),
        ],
        tenant_index,
        [inner_input, tenant_scale, step_size, decay_rate[None]],
    )


    w_all, weighted_t, logs = lax.optimization_barrier((w_all, weighted_t, logs))

    size = HALO + Q
    sums = kernel_call(
        project_kernel,
        shape((n_x, lax.axis_size("core"), size, 2 * N), bf16),
        None,
        [*w_all, rows],
        [
            pltpu.VMEM((w_zh.shape[0] * QUAD, depth), bf16),
            pltpu.VMEM((n_x * size, depth), bf16),
        ],
    )
    sums = swap(sums.reshape(-1, size, 2 * N), TP)
    sums = to_owner(kernel_call(sum_kernel, shape((size, 2 * N), bf16), None, [sums]))
    keys, update = kernel_call(
        keys_kernel,
        [shape((Q, 2 * N), bf16), shape((heads, head_width + LOG_ROWS, N), bf16)],
        None,
        [sums, conv_taps, weighted_t, logs],
    )

    got = swap(update, NEAR)
    total = kernel_call(
        total_kernel, shape((n_x * head_width + LOG_ROWS, N), bf16), None, [got]
    )
    states = kernel_call(
        states_kernel,
        shape((heads, head_width, N), bf16),
        None,
        [lax.all_gather(total, "zh"), got],
    )
    start = swap(states, NEAR).reshape(width, N)

    mixed, grown = kernel_call(
        within_kernel,
        [shape((Q, width), f32)] * 2,
        tenant_index,
        [keys, driven, cum, cum_t, inner_input, tenant_scale, skip_gain[None], gate_input],
    )
    return kernel_call(
        output_kernel,
        shape((Q, width), bf16),
        None,
        [keys, start, mixed, grown, norm_gain[None]],
    )


def solution(mesh):
    fine = Mesh(mesh.devices.reshape(4, 4, 4, 4, 2), CTX + TP)
    in_specs = (
        P(CTX, TP),
        P(TP, CTX),
        P(None, TP),
        P(CTX, TP),
        P(CTX, TP),
        P(CTX, TP),
        P(TP),
        P(TP),
        P(None, TP),
        P(CTX),
        P(TP),
    )
    return jax.shard_map(
        per_device, mesh=fine, in_specs=in_specs, out_specs=P(CTX, TP), check_vma=False
    )
```

```python
import jax
import jax.numpy as jnp
from jax import lax
from jax.experimental import pallas as pl
from jax.experimental.pallas import tpu as pltpu
from jax.sharding import Mesh, PartitionSpec as P

N = 128
Q = 128
QUAD = 4
HALO = 16
REACH = 3
LOG_ROWS = 16
Z = ("zh", "zl")
CTX = ("x",) + Z
NEAR = ("x", "zl")
TP = ("y", "core")

epsilon = 1e-05
bf16 = jnp.bfloat16
f32 = jnp.float32
EXACT = lax.Precision.HIGHEST

VMEM = pl.BlockSpec(memory_space=pltpu.VMEM)
SMEM = pl.BlockSpec(memory_space=pltpu.SMEM)


def swap(blocks, axis):
    return lax.all_to_all(blocks, axis, 0, 0, tiled=True)


def share(block, axis):
    peers = lax.axis_size(axis)
    return swap(jnp.broadcast_to(block[None], (peers,) + block.shape), axis)


def to_owner(block):
    side = lax.axis_size("x")
    pairs = [
        (i * side + j, (j + side // 2) % side * side + i) for i in range(side) for j in range(side)
    ]
    return lax.ppermute(block, ("x", "y"), pairs)


def shape(dims, kind):
    return jax.ShapeDtypeStruct(dims, kind)


def kernel_call(body, outs, scalars, args, scratch=(), flops=1_000_000):
    placed = [] if scalars is None else [scalars]
    return pl.pallas_call(
        body,
        out_shape=outs,
        in_specs=[SMEM] * len(placed) + [VMEM] * len(args),
        out_specs=jax.tree.map(lambda _: VMEM, outs),
        scratch_shapes=scratch,
        compiler_params=pltpu.CompilerParams(vmem_limit_bytes=32 * 1024 * 1024),
        cost_estimate=pl.CostEstimate(flops=flops, bytes_accessed=1_000_000, transcendentals=0),
    )(*placed, *args)


def expand(columns, head_width):
    heads = columns.shape[1]
    shape2 = (heads, heads * head_width)
    head = lax.broadcasted_iota(jnp.int32, shape2, 0)
    lane = lax.broadcasted_iota(jnp.int32, shape2, 1)
    first = head * head_width
    onehot = jnp.where((lane >= first) & (lane < first + head_width), 1.0, 0.0)
    return jnp.dot(columns, onehot, precision=EXACT, preferred_element_type=f32)


def split3(row):
    hi = row.astype(bf16).astype(f32)
    mid = (row - hi).astype(bf16).astype(f32)
    return hi, mid, row - hi - mid


def log_rows(row):
    hi, mid, low = split3(row)
    at = lax.broadcasted_iota(jnp.int32, (LOG_ROWS, row.shape[1]), 0)
    rows = jnp.where(at == 0, hi, jnp.where(at == 1, mid, jnp.where(at == 2, low, 0.0)))
    return rows.astype(bf16)


def log_row(rows):
    return jnp.sum(rows.astype(f32), axis=0, keepdims=True)


def scaled_by_tenant(tenant, inner_ref, scale_ref):
    row = lax.broadcasted_iota(jnp.int32, scale_ref.shape, 0)
    chosen = jnp.where(row == tenant, scale_ref[...].astype(f32), 0.0)
    return inner_ref[...].astype(f32) * jnp.sum(chosen, axis=0, keepdims=True)


def drive_kernel(
    tenant, inner, scale, step, decay, skip, gate, gain, driven, cum, cum_t, weighted_t, logs,
    skipped, gates, grown, gains,
):
    heads = step.shape[1]
    head_width = inner.shape[1] // heads
    log_decay = -step[...] * decay[...]
    rows = lax.broadcasted_iota(jnp.int32, (Q, Q), 0)
    cols = lax.broadcasted_iota(jnp.int32, (Q, Q), 1)
    lower = jnp.where(rows >= cols, 1.0, 0.0)
    so_far = jnp.dot(lower, log_decay, precision=EXACT, preferred_element_type=f32)
    cum[...] = so_far
    cum_t[...] = lax.dot_general(
        so_far,
        jnp.where(rows == cols, 1.0, 0.0),
        (((0,), (0,)), ((), ())),
        precision=EXACT,
        preferred_element_type=f32,
    )
    end = so_far[Q - 1 :]
    scaled = scaled_by_tenant(tenant[0], inner, scale)
    drive = (scaled * expand(step[...], head_width)).astype(bf16)
    driven[...] = drive
    tail = expand(jnp.exp(end - so_far), head_width)
    weighted_t[...] = jnp.transpose(tail * drive.astype(f32)).astype(bf16)
    g = gate[...].astype(f32)
    g = g / (1.0 + jnp.exp(-g))
    gates[...] = g
    skipped[...] = expand(skip[...], head_width) * scaled * g
    grown[...] = expand(jnp.exp(so_far), head_width) * g
    gains[...] = gain[...].astype(f32)
    for h in range(heads):
        logs[h] = log_rows(jnp.broadcast_to(end[:, h : h + 1], (1, N)))


def share_kernel(block, out, held, arrived, sent):
    fetch = pltpu.make_async_copy(block, held, arrived)
    fetch.start()
    fetch.wait()
    copies = [pltpu.make_async_copy(held, out.at[i], sent.at[i]) for i in range(out.shape[0])]
    for copy in copies:
        copy.start()
    for copy in copies:
        copy.wait()


def project_kernel(own, one, other, across, rows, out, w_in_order, all_rows):
    n_part = N // QUAD
    halves = own.shape[0] // n_part
    zh, zl, core = (lax.axis_index(a) for a in Z + ("core",))
    steps = (0, 2 * core - 1, 1 - 2 * core, 2)
    for w, step in zip((own, one, other, across), steps):
        s = lax.rem(zl + step + QUAD, QUAD)
        for i in range(halves):
            at = pl.multiple_of(i * N + s * n_part, n_part)
            w_in_order[pl.ds(at, n_part)] = w[i * n_part : (i + 1) * n_part]
    packed = jnp.where(
        core == 0, one[halves * n_part :].astype(f32), other[halves * n_part :].astype(f32)
    )
    tails = [
        pltpu.roll(packed, (HALO - (i + 1) * REACH) % HALO, 0).astype(bf16)
        for i in range(rows.shape[0])
    ]
    first = (zh == 0) & (zl == 0)
    size = HALO + Q
    for block in range(rows.shape[0]):
        behind = tails[block - 1] if block > 0 else jnp.zeros_like(tails[0])
        all_rows[block * size : block * size + HALO] = jnp.where(first, behind, tails[block])
        all_rows[block * size + HALO : (block + 1) * size] = rows[block]
    for c in range(out.shape[1]):
        sums = lax.dot_general(
            all_rows[...],
            w_in_order[c * 2 * N : (c + 1) * 2 * N],
            (((1,), (1,)), ((), ())),
            preferred_element_type=f32,
        ).astype(bf16)
        for block in range(rows.shape[0]):
            to = (block + rows.shape[0] // 2) % rows.shape[0]
            out[to, c] = sums[block * size : (block + 1) * size]


def sum_kernel(parts, out):
    raw = parts[0].astype(f32)
    for i in range(1, parts.shape[0]):
        raw = raw + parts[i].astype(f32)
    out[...] = raw.astype(bf16)


def keys_kernel(sums, taps, weighted_t, logs, keys_out, out):
    raw = sums[...].astype(f32)
    n_taps = taps.shape[0]
    summed = taps[n_taps - 1 :] * raw[HALO:]
    for d in range(1, n_taps):
        summed = summed + taps[n_taps - 1 - d : n_taps - d] * raw[HALO - d : HALO - d + Q]
    keys = (summed / (1.0 + jnp.exp(-summed))).astype(bf16)
    keys_out[...] = keys
    update = jnp.dot(weighted_t[...], keys[:, :N], preferred_element_type=f32).astype(bf16)
    heads = out.shape[0]
    head_width = update.shape[0] // heads
    for h in range(heads):
        out[h, :head_width] = update[h * head_width : (h + 1) * head_width]
        out[h, head_width:] = logs[h]


def total_kernel(got, total):
    head_width = got.shape[1] - LOG_ROWS
    rows = got.shape[0] // QUAD
    at = lax.broadcasted_iota(jnp.int32, (LOG_ROWS, N), 0)
    logs = jnp.zeros((LOG_ROWS, N), f32)
    for row in range(rows):
        acc = jnp.zeros((head_width, N), f32)
        log_acc = jnp.zeros((1, N), f32)
        for b in range(QUAD):
            log = log_row(got[row * QUAD + b, head_width:])
            acc = jnp.exp(log) * acc + got[row * QUAD + b, :head_width].astype(f32)
            log_acc = log_acc + log
        total[row * head_width : (row + 1) * head_width] = acc.astype(bf16)
        for i, part in enumerate(split3(log_acc)):
            logs = jnp.where(at == row * 3 + i, part, logs)
    total[rows * head_width :] = logs.astype(bf16)


def states_kernel(totals, got, out):
    zh = lax.axis_index("zh")
    head_width = out.shape[1]
    rows = out.shape[0] // QUAD
    logs = [totals[quad, rows * head_width :].astype(f32) for quad in range(totals.shape[0])]
    acc = jnp.zeros((head_width, N), f32)
    for row in range(rows):
        carry = acc
        for quad in range(totals.shape[0]):
            carry = jnp.where(zh == quad, acc, carry)
            log = jnp.sum(logs[quad][3 * row : 3 * row + 3], axis=0, keepdims=True)
            update = totals[quad, row * head_width : (row + 1) * head_width]
            acc = jnp.exp(log) * acc + update.astype(f32)
        for b in range(QUAD):
            at = row * QUAD + b
            out[at] = carry.astype(bf16)
            if b < QUAD - 1:
                log = log_row(got[at, head_width:])
                carry = jnp.exp(log) * carry + got[at, :head_width].astype(f32)


def output_kernel(
    keys, start, driven, cum, cum_t, skipped, gates, grown, gain, out
):
    scores = lax.dot_general(
        keys[:, N:], keys[:, :N], (((1,), (1,)), ((), ())), preferred_element_type=f32
    )
    rows = lax.broadcasted_iota(jnp.int32, (Q, Q), 0)
    cols = lax.broadcasted_iota(jnp.int32, (Q, Q), 1)
    causal = rows >= cols
    heads = cum.shape[1]
    width = out.shape[1]
    head_width = width // heads
    per_tile = Q // head_width
    gated = []
    squares = jnp.zeros((Q, 1), f32)
    for tile in range(heads // per_tile):
        at = slice(tile * Q, (tile + 1) * Q)
        mixed = None
        for i in range(per_tile):
            h = tile * per_tile + i
            lag = cum[:, h : h + 1] - cum_t[h : h + 1]
            weights = jnp.where(causal, scores * jnp.exp(jnp.where(causal, lag, 0.0)), 0.0)
            summed = jnp.dot(weights.astype(bf16), driven[:, at], preferred_element_type=f32)
            mixed = summed if mixed is None else jnp.where(cols < i * head_width, mixed, summed)
        carried = lax.dot_general(
            keys[:, N:], start[at], (((1,), (1,)), ((), ())), preferred_element_type=f32
        )
        value = mixed * gates[:, at] + skipped[:, at] + grown[:, at] * carried
        squares = squares + jnp.sum(value * value, axis=1, keepdims=True)
        gated.append(value)
    inverse = lax.rsqrt(squares / width + epsilon)
    for tile, value in enumerate(gated):
        at = slice(tile * Q, (tile + 1) * Q)
        out[:, at] = (value * inverse * gain[:, at]).astype(bf16)


def per_device(
    hidden_states,
    select_weight,
    conv_taps,
    inner_input,
    gate_input,
    step_size,
    decay_rate,
    skip_gain,
    tenant_scale,
    tenant_index,
    norm_gain,
):
    heads = decay_rate.shape[0]
    width = inner_input.shape[1]
    head_width = width // heads
    n_z = lax.axis_size(Z)
    n_x = lax.axis_size("x")
    depth = hidden_states.shape[1]

    rows = pl.pallas_call(
        share_kernel,
        out_shape=shape((n_x,) + hidden_states.shape, bf16),
        in_specs=[pl.BlockSpec(memory_space=pl.ANY)],
        out_specs=pl.BlockSpec(memory_space=pl.ANY),
        scratch_shapes=[
            pltpu.VMEM(hidden_states.shape, bf16),
            pltpu.SemaphoreType.DMA,
            pltpu.SemaphoreType.DMA((n_x,)),
        ],
        cost_estimate=pl.CostEstimate(flops=0, bytes_accessed=1_000_000, transcendentals=0),
    )(hidden_states)
    rows = swap(rows, "x")

    n_part = select_weight.shape[1]
    w_zh = lax.all_gather(select_weight.T, "zh", axis=0, tiled=True)
    w_zh, rows = lax.optimization_barrier((w_zh, rows))
    n_core = lax.axis_size("core")
    tails = jnp.pad(
        rows[:, Q - REACH :].reshape(n_x * REACH, depth), ((0, HALO - n_x * REACH), (0, 0))
    )
    both = jnp.concatenate([w_zh, tails], axis=0)

    def from_side(block, step):
        pairs = [
            (i * n_core + c, (i + step * (1 - 2 * c)) % n_z * n_core + c)
            for i in range(n_z)
            for c in range(n_core)
        ]
        return lax.ppermute(block, Z + ("core",), pairs)

    w_all = [w_zh, from_side(both, 1), from_side(both, -1), from_side(w_zh, 2)]

    driven, cum, cum_t, weighted_t, logs, skipped, gates, grown, gains = kernel_call(
        drive_kernel,
        [
            shape((Q, width), bf16),
            shape((Q, heads), f32),
            shape((heads, Q), f32),
            shape((width, Q), bf16),
            shape((heads, LOG_ROWS, N), bf16),
            shape((Q, width), f32),
            shape((Q, width), f32),
            shape((Q, width), f32),
            shape((1, width), f32),
        ],
        tenant_index,
        [
            inner_input,
            tenant_scale,
            step_size,
            decay_rate[None],
            skip_gain[None],
            gate_input,
            norm_gain[None],
        ],
    )


    w_all, weighted_t, logs = lax.optimization_barrier((w_all, weighted_t, logs))

    size = HALO + Q
    sums = kernel_call(
        project_kernel,
        shape((n_x, lax.axis_size("core"), size, 2 * N), bf16),
        None,
        [*w_all, rows],
        [
            pltpu.VMEM((w_zh.shape[0] * QUAD, depth), bf16),
            pltpu.VMEM((n_x * size, depth), bf16),
        ],
    )
    sums = swap(sums.reshape(-1, size, 2 * N), TP)
    sums = to_owner(kernel_call(sum_kernel, shape((size, 2 * N), bf16), None, [sums]))
    keys, update = kernel_call(
        keys_kernel,
        [shape((Q, 2 * N), bf16), shape((heads, head_width + LOG_ROWS, N), bf16)],
        None,
        [sums, conv_taps, weighted_t, logs],
    )

    got = swap(update, NEAR)
    total = kernel_call(
        total_kernel, shape((n_x * head_width + LOG_ROWS, N), bf16), None, [got]
    )
    states = kernel_call(
        states_kernel,
        shape((heads, head_width, N), bf16),
        None,
        [lax.all_gather(total, "zh"), got],
    )
    start = swap(states, NEAR).reshape(width, N)

    return kernel_call(
        output_kernel,
        shape((Q, width), bf16),
        None,
        [keys, start, driven, cum, cum_t, skipped, gates, grown, gains],
    )


def solution(mesh):
    fine = Mesh(mesh.devices.reshape(4, 4, 4, 4, 2), CTX + TP)
    in_specs = (
        P(CTX, TP),
        P(TP, CTX),
        P(None, TP),
        P(CTX, TP),
        P(CTX, TP),
        P(CTX, TP),
        P(TP),
        P(TP),
        P(None, TP),
        P(CTX),
        P(TP),
    )
    return jax.shard_map(
        per_device, mesh=fine, in_specs=in_specs, out_specs=P(CTX, TP), check_vma=False
    )
```

```python
import jax
import jax.numpy as jnp
from jax import lax
from jax.experimental import pallas as pl
from jax.experimental.pallas import tpu as pltpu
from jax.sharding import Mesh, PartitionSpec as P

N = 128
Q = 128
QUAD = 4
HALO = 16
REACH = 3
LOG_ROWS = 16
Z = ("zh", "zl")
CTX = ("x",) + Z
NEAR = ("x", "zl")
TP = ("y", "core")

epsilon = 1e-05
bf16 = jnp.bfloat16
f32 = jnp.float32
EXACT = lax.Precision.HIGHEST

VMEM = pl.BlockSpec(memory_space=pltpu.VMEM)
SMEM = pl.BlockSpec(memory_space=pltpu.SMEM)


def swap(blocks, axis):
    return lax.all_to_all(blocks, axis, 0, 0, tiled=True)


def share(block, axis):
    peers = lax.axis_size(axis)
    return swap(jnp.broadcast_to(block[None], (peers,) + block.shape), axis)


def to_owner(block):
    side = lax.axis_size("x")
    pairs = [
        (i * side + j, (j + side // 2) % side * side + i) for i in range(side) for j in range(side)
    ]
    return lax.ppermute(block, ("x", "y"), pairs)


def shape(dims, kind):
    return jax.ShapeDtypeStruct(dims, kind)


def kernel_call(body, outs, scalars, args, scratch=(), flops=1_000_000):
    placed = [] if scalars is None else [scalars]
    return pl.pallas_call(
        body,
        out_shape=outs,
        in_specs=[SMEM] * len(placed) + [VMEM] * len(args),
        out_specs=jax.tree.map(lambda _: VMEM, outs),
        scratch_shapes=scratch,
        compiler_params=pltpu.CompilerParams(vmem_limit_bytes=32 * 1024 * 1024),
        cost_estimate=pl.CostEstimate(flops=flops, bytes_accessed=1_000_000, transcendentals=0),
    )(*placed, *args)


def expand(columns, head_width):
    heads = columns.shape[1]
    shape2 = (heads, heads * head_width)
    head = lax.broadcasted_iota(jnp.int32, shape2, 0)
    lane = lax.broadcasted_iota(jnp.int32, shape2, 1)
    first = head * head_width
    onehot = jnp.where((lane >= first) & (lane < first + head_width), 1.0, 0.0)
    return jnp.dot(columns, onehot, precision=EXACT, preferred_element_type=f32)


def split3(row):
    hi = row.astype(bf16).astype(f32)
    mid = (row - hi).astype(bf16).astype(f32)
    return hi, mid, row - hi - mid


def log_rows(row):
    hi, mid, low = split3(row)
    at = lax.broadcasted_iota(jnp.int32, (LOG_ROWS, row.shape[1]), 0)
    rows = jnp.where(at == 0, hi, jnp.where(at == 1, mid, jnp.where(at == 2, low, 0.0)))
    return rows.astype(bf16)


def log_row(rows):
    return jnp.sum(rows.astype(f32), axis=0, keepdims=True)


def scaled_by_tenant(tenant, inner_ref, scale_ref):
    row = lax.broadcasted_iota(jnp.int32, scale_ref.shape, 0)
    chosen = jnp.where(row == tenant, scale_ref[...].astype(f32), 0.0)
    return inner_ref[...].astype(f32) * jnp.sum(chosen, axis=0, keepdims=True)


def drive_kernel(tenant, inner, scale, step, decay, driven, cum, cum_t, weighted_t, logs):
    heads = step.shape[1]
    head_width = inner.shape[1] // heads
    log_decay = -step[...] * decay[...]
    rows = lax.broadcasted_iota(jnp.int32, (Q, Q), 0)
    cols = lax.broadcasted_iota(jnp.int32, (Q, Q), 1)
    lower = jnp.where(rows >= cols, 1.0, 0.0)
    so_far = jnp.dot(lower, log_decay, precision=EXACT, preferred_element_type=f32)
    cum[...] = so_far
    cum_t[...] = lax.dot_general(
        so_far,
        jnp.where(rows == cols, 1.0, 0.0),
        (((0,), (0,)), ((), ())),
        precision=EXACT,
        preferred_element_type=f32,
    )
    end = so_far[Q - 1 :]
    scaled = scaled_by_tenant(tenant[0], inner, scale)
    drive = (scaled * expand(step[...], head_width)).astype(bf16)
    driven[...] = drive
    tail = expand(jnp.exp(end - so_far), head_width)
    weighted_t[...] = jnp.transpose(tail * drive.astype(f32)).astype(bf16)
    for h in range(heads):
        logs[h] = log_rows(jnp.broadcast_to(end[:, h : h + 1], (1, N)))


def share_kernel(block, out, held, arrived, sent):
    fetch = pltpu.make_async_copy(block, held, arrived)
    fetch.start()
    fetch.wait()
    copies = [pltpu.make_async_copy(held, out.at[i], sent.at[i]) for i in range(out.shape[0])]
    for copy in copies:
        copy.start()
    for copy in copies:
        copy.wait()


def project_kernel(own, one, other, across, rows, out, w_in_order, all_rows):
    n_part = N // QUAD
    halves = own.shape[0] // n_part
    zh, zl, core = (lax.axis_index(a) for a in Z + ("core",))
    steps = (0, 2 * core - 1, 1 - 2 * core, 2)
    for w, step in zip((own, one, other, across), steps):
        s = lax.rem(zl + step + QUAD, QUAD)
        for i in range(halves):
            at = pl.multiple_of(i * N + s * n_part, n_part)
            w_in_order[pl.ds(at, n_part)] = w[i * n_part : (i + 1) * n_part]
    packed = jnp.where(
        core == 0, one[halves * n_part :].astype(f32), other[halves * n_part :].astype(f32)
    )
    tails = [
        pltpu.roll(packed, (HALO - (i + 1) * REACH) % HALO, 0).astype(bf16)
        for i in range(rows.shape[0])
    ]
    first = (zh == 0) & (zl == 0)
    size = HALO + Q
    for block in range(rows.shape[0]):
        behind = tails[block - 1] if block > 0 else jnp.zeros_like(tails[0])
        all_rows[block * size : block * size + HALO] = jnp.where(first, behind, tails[block])
        all_rows[block * size + HALO : (block + 1) * size] = rows[block]
    for c in range(out.shape[1]):
        sums = lax.dot_general(
            all_rows[...],
            w_in_order[c * 2 * N : (c + 1) * 2 * N],
            (((1,), (1,)), ((), ())),
            preferred_element_type=f32,
        ).astype(bf16)
        for block in range(rows.shape[0]):
            to = (block + rows.shape[0] // 2) % rows.shape[0]
            out[to, c] = sums[block * size : (block + 1) * size]


def sum_kernel(parts, out):
    raw = parts[0].astype(f32)
    for i in range(1, parts.shape[0]):
        raw = raw + parts[i].astype(f32)
    out[...] = raw.astype(bf16)


def keys_kernel(sums, taps, weighted_t, logs, keys_out, out):
    raw = sums[...].astype(f32)
    n_taps = taps.shape[0]
    summed = taps[n_taps - 1 :] * raw[HALO:]
    for d in range(1, n_taps):
        summed = summed + taps[n_taps - 1 - d : n_taps - d] * raw[HALO - d : HALO - d + Q]
    keys = (summed / (1.0 + jnp.exp(-summed))).astype(bf16)
    keys_out[...] = keys
    update = jnp.dot(weighted_t[...], keys[:, :N], preferred_element_type=f32).astype(bf16)
    heads = out.shape[0]
    head_width = update.shape[0] // heads
    for h in range(heads):
        out[h, :head_width] = update[h * head_width : (h + 1) * head_width]
        out[h, head_width:] = logs[h]


def total_kernel(got, total):
    head_width = got.shape[1] - LOG_ROWS
    rows = got.shape[0] // QUAD
    at = lax.broadcasted_iota(jnp.int32, (LOG_ROWS, N), 0)
    logs = jnp.zeros((LOG_ROWS, N), f32)
    for row in range(rows):
        acc = jnp.zeros((head_width, N), f32)
        log_acc = jnp.zeros((1, N), f32)
        for b in range(QUAD):
            log = log_row(got[row * QUAD + b, head_width:])
            acc = jnp.exp(log) * acc + got[row * QUAD + b, :head_width].astype(f32)
            log_acc = log_acc + log
        total[row * head_width : (row + 1) * head_width] = acc.astype(bf16)
        for i, part in enumerate(split3(log_acc)):
            logs = jnp.where(at == row * 3 + i, part, logs)
    total[rows * head_width :] = logs.astype(bf16)


def states_kernel(totals, got, out):
    zh = lax.axis_index("zh")
    head_width = out.shape[1]
    rows = out.shape[0] // QUAD
    logs = [totals[quad, rows * head_width :].astype(f32) for quad in range(totals.shape[0])]
    acc = jnp.zeros((head_width, N), f32)
    for row in range(rows):
        carry = acc
        for quad in range(totals.shape[0]):
            carry = jnp.where(zh == quad, acc, carry)
            log = jnp.sum(logs[quad][3 * row : 3 * row + 3], axis=0, keepdims=True)
            update = totals[quad, row * head_width : (row + 1) * head_width]
            acc = jnp.exp(log) * acc + update.astype(f32)
        for b in range(QUAD):
            at = row * QUAD + b
            out[at] = carry.astype(bf16)
            if b < QUAD - 1:
                log = log_row(got[at, head_width:])
                carry = jnp.exp(log) * carry + got[at, :head_width].astype(f32)


def within_kernel(tenant, keys, driven, cum, cum_t, inner, scale, skip, gate, out, grown):
    scores = lax.dot_general(
        keys[:, N:], keys[:, :N], (((1,), (1,)), ((), ())), preferred_element_type=f32
    )
    rows = lax.broadcasted_iota(jnp.int32, (Q, Q), 0)
    cols = lax.broadcasted_iota(jnp.int32, (Q, Q), 1)
    causal = rows >= cols
    heads = cum.shape[1]
    head_width = driven.shape[1] // heads
    per_tile = Q // head_width
    skipped = expand(skip[...], head_width) * scaled_by_tenant(tenant[0], inner, scale)
    g = gate[...].astype(f32)
    gates = g / (1.0 + jnp.exp(-g))
    grown[...] = gates * expand(jnp.exp(cum[...]), head_width)
    for tile in range(heads // per_tile):
        at = slice(tile * Q, (tile + 1) * Q)
        mixed = None
        for i in range(per_tile):
            h = tile * per_tile + i
            lag = cum[:, h : h + 1] - cum_t[h : h + 1]
            weights = jnp.where(causal, scores * jnp.exp(jnp.where(causal, lag, 0.0)), 0.0)
            summed = jnp.dot(weights.astype(bf16), driven[:, at], preferred_element_type=f32)
            mixed = summed if mixed is None else jnp.where(cols < i * head_width, mixed, summed)
        out[:, at] = (mixed + skipped[:, at]) * gates[:, at]


def output_kernel(keys, start, mixed, grown, gain, out):
    width = out.shape[1]
    quarter = width // QUAD
    gated = []
    squares = jnp.zeros((Q, 1), f32)
    for q in range(QUAD):
        at = slice(q * quarter, (q + 1) * quarter)
        carried = lax.dot_general(
            keys[:, N:], start[at], (((1,), (1,)), ((), ())), preferred_element_type=f32
        )
        value = mixed[:, at] + grown[:, at] * carried
        squares = squares + jnp.sum(value * value, axis=1, keepdims=True)
        gated.append(value)
    inverse = lax.rsqrt(squares / width + epsilon)
    for q in range(QUAD):
        at = slice(q * quarter, (q + 1) * quarter)
        out[:, at] = (gated[q] * inverse * gain[:, at].astype(f32)).astype(bf16)


def per_device(
    hidden_states,
    select_weight,
    conv_taps,
    inner_input,
    gate_input,
    step_size,
    decay_rate,
    skip_gain,
    tenant_scale,
    tenant_index,
    norm_gain,
):
    heads = decay_rate.shape[0]
    width = inner_input.shape[1]
    head_width = width // heads
    n_z = lax.axis_size(Z)
    n_x = lax.axis_size("x")
    depth = hidden_states.shape[1]

    rows = pl.pallas_call(
        share_kernel,
        out_shape=shape((n_x,) + hidden_states.shape, bf16),
        in_specs=[pl.BlockSpec(memory_space=pl.ANY)],
        out_specs=pl.BlockSpec(memory_space=pl.ANY),
        scratch_shapes=[
            pltpu.VMEM(hidden_states.shape, bf16),
            pltpu.SemaphoreType.DMA,
            pltpu.SemaphoreType.DMA((n_x,)),
        ],
        cost_estimate=pl.CostEstimate(flops=0, bytes_accessed=1_000_000, transcendentals=0),
    )(hidden_states)
    rows = swap(rows, "x")

    n_part = select_weight.shape[1]
    w_zh = lax.all_gather(select_weight.T, "zh", axis=0, tiled=True)
    w_zh, rows = lax.optimization_barrier((w_zh, rows))
    n_core = lax.axis_size("core")
    tails = jnp.pad(
        rows[:, Q - REACH :].reshape(n_x * REACH, depth), ((0, HALO - n_x * REACH), (0, 0))
    )
    both = jnp.concatenate([w_zh, tails], axis=0)

    def from_side(block, step):
        pairs = [
            (i * n_core + c, (i + step * (1 - 2 * c)) % n_z * n_core + c)
            for i in range(n_z)
            for c in range(n_core)
        ]
        return lax.ppermute(block, Z + ("core",), pairs)

    w_all = [w_zh, from_side(both, 1), from_side(both, -1), from_side(w_zh, 2)]

    size = HALO + Q
    sums = kernel_call(
        project_kernel,
        shape((n_x, lax.axis_size("core"), size, 2 * N), bf16),
        None,
        [*w_all, rows],
        [
            pltpu.VMEM((w_zh.shape[0] * QUAD, depth), bf16),
            pltpu.VMEM((n_x * size, depth), bf16),
        ],
    )
    sums = swap(sums.reshape(-1, size, 2 * N), TP)
    sums, step_late = lax.optimization_barrier((sums, step_size))
    sums = to_owner(kernel_call(sum_kernel, shape((size, 2 * N), bf16), None, [sums]))

    driven, cum, cum_t, weighted_t, logs = kernel_call(
        drive_kernel,
        [
            shape((Q, width), bf16),
            shape((Q, heads), f32),
            shape((heads, Q), f32),
            shape((width, Q), bf16),
            shape((heads, LOG_ROWS, N), bf16),
        ],
        tenant_index,
        [inner_input, tenant_scale, step_late, decay_rate[None]],
    )

    keys, update = kernel_call(
        keys_kernel,
        [shape((Q, 2 * N), bf16), shape((heads, head_width + LOG_ROWS, N), bf16)],
        None,
        [sums, conv_taps, weighted_t, logs],
    )

    got = swap(update, NEAR)
    total = kernel_call(
        total_kernel, shape((n_x * head_width + LOG_ROWS, N), bf16), None, [got]
    )
    states = kernel_call(
        states_kernel,
        shape((heads, head_width, N), bf16),
        None,
        [lax.all_gather(total, "zh"), got],
    )
    start = swap(states, NEAR).reshape(width, N)

    mixed, grown = kernel_call(
        within_kernel,
        [shape((Q, width), f32)] * 2,
        tenant_index,
        [keys, driven, cum, cum_t, inner_input, tenant_scale, skip_gain[None], gate_input],
    )
    return kernel_call(
        output_kernel,
        shape((Q, width), bf16),
        None,
        [keys, start, mixed, grown, norm_gain[None]],
    )


def solution(mesh):
    fine = Mesh(mesh.devices.reshape(4, 4, 4, 4, 2), CTX + TP)
    in_specs = (
        P(CTX, TP),
        P(TP, CTX),
        P(None, TP),
        P(CTX, TP),
        P(CTX, TP),
        P(CTX, TP),
        P(TP),
        P(TP),
        P(None, TP),
        P(CTX),
        P(TP),
    )
    return jax.shard_map(
        per_device, mesh=fine, in_specs=in_specs, out_specs=P(CTX, TP), check_vma=False
    )
```
